256 devices in a mesh: lon: 32 (over y_hi, z, core), batch: 8 (over y_lo, x).
Axes of the slice: x: 4, y: 4 (y_hi: 2, y_lo: 2; y = y_hi * 2 + y_lo), z: 8, core: 2. Of those that a mesh axis runs over, the one named last changes fastest.
Arguments:
- images: bfloat16 [8, 128, 512, 128], P('batch', None, 'lon'), may hold values from -6 to 6
- weights: bfloat16 [4, 9, 128, 128], replicated, may hold values from -0.3125 to 0.3125
- cotangent: bfloat16 [8, 128, 512, 128], P('batch', None, 'lon'), may hold values from -6 to 6
Outputs:
- features: bfloat16 [8, 128, 512, 128], P('batch', None, 'lon')
- image_grads: bfloat16 [8, 128, 512, 128], P('batch', None, 'lon')
- weight_grads: float32 [4, 1152, 128], P(None, 'lon', 'batch')
The draws below stay inside these ranges and needn't reach their ends.
All inputs are finite; a program needn't handle non-finite values.
Results may differ from the reference program's by a relative error of at most 0.035.
Values may be sent and summed in bfloat16 or wider, within the bound.
A program may use at most 128 MiB of HBM per device.

```python
import math
import jax
import jax.numpy as jnp
from jax import lax

C = 128
LAYERS = 4
LAT = 128
BATCH = 8
WIDTH = 512


def strengthened(entries, rng, source, target, blocks, factor):
    owner, partner = [(jnp.arange(entries.shape[dim]) // (entries.shape[dim] // blocks)).reshape([-1 if axis == dim else 1 for axis in range(entries.ndim)]) for dim in (source, target)]
    chosen = jax.random.permutation(rng, blocks)[partner]
    strong = (owner == chosen) | (owner == (partner + blocks // 2) % blocks)
    return jnp.where(strong, factor * entries, entries)


def level_of(own_key, dims, cuts, smallest, high):
    def one(dim, shards_of):
        draws = jax.random.uniform(jax.random.fold_in(jax.random.fold_in(own_key, 6), dim), (shards_of,), jnp.float32, smallest / len(cuts), high / len(cuts))
        return jnp.repeat(jnp.exp(draws), dims[dim] // shards_of).reshape((-1,) + (1,) * (len(dims) - dim - 1))

    loudness = one(*cuts[0])
    for cut in cuts[1:]:
        loudness = loudness * one(*cut)
    return loudness


def scatter_about(key, shape, spread, bound, shards=(), dtype=jnp.bfloat16):
    values = spread * jax.random.normal(key, shape, jnp.float32)
    if shards:
        values = values * level_of(key, shape, shards, -0.22, 0.18)
    return jnp.clip(values, -bound, bound).astype(dtype)


def gaussian_with(rng, dims, spread, limit, split, heavy, kind=jnp.bfloat16):
    array = spread * jax.random.normal(rng, dims, jnp.float32)
    if split:
        array = array * level_of(rng, dims, split, -0.22, 0.18)
    return jnp.clip(strengthened(array, jax.random.fold_in(rng, 3), *heavy), -limit, limit).astype(kind)


def setup_inputs(seed: int = 0) -> dict:
    splits = jax.random.split(jax.random.key(seed), 4)
    images = scatter_about(splits[0], (BATCH, LAT, WIDTH, C), 1.0, 6.0, ((0, 8), (2, 32)))
    weights = scatter_about(splits[1], (LAYERS, 9, C, C), (3 * C) ** -0.5, 0.3125)
    cotangent = gaussian_with(splits[2], (BATCH, LAT, WIDTH, C), 1.0, 6.0, ((0, 8), (2, 32)), (2, 3, 32, 2.75))
    return {"images": images, "weights": weights, "cotangent": cotangent}


def gather_taps(field, dilation):
    height = field.shape[0]
    width_all = field.shape[1]
    padded = jnp.pad(field, ((dilation, dilation), (0, 0), (0, 0)))
    padded = jnp.concatenate([padded[:, width_all - dilation:], padded, padded[:, :dilation]], axis=1)
    pieces = [padded[dilation + vertical * dilation:dilation + vertical * dilation + height, dilation + horizontal * dilation:dilation + horizontal * dilation + width_all] for vertical in (-1, 0, 1) for horizontal in (-1, 0, 1)]
    return jnp.concatenate(pieces, axis=-1).reshape(height * width_all, -1)

def slope(pre):
    value = pre.astype(jnp.float32)
    sigma = jax.nn.sigmoid(value)
    return sigma * (1.0 + value * (1.0 - sigma))

def reference(images, weights, cotangent):
    channels = weights.shape[-1]
    stacked = weights.reshape(LAYERS, 9 * channels, channels)
    flipped = jnp.transpose(weights[:, ::-1], (0, 1, 3, 2)).reshape(LAYERS, 9 * channels, channels)

    def one_image(totals, inputs):
        picture, upstream = inputs
        height, width_all = (picture.shape[0], picture.shape[1])
        levels = [picture]
        preacts = []
        for number in range(LAYERS):
            dilation = 2 ** number
            summed = jnp.dot(gather_taps(levels[-1], dilation), stacked[number], preferred_element_type=jnp.float32)
            summed = summed.reshape(height, width_all, channels)
            preacts.append(summed.astype(jnp.bfloat16))
            levels.append(jax.nn.silu(summed).astype(jnp.bfloat16))
        signal = (upstream.astype(jnp.float32) * slope(preacts[-1])).astype(jnp.bfloat16)
        gradients = []
        input_grad = None
        for number in reversed(range(LAYERS)):
            dilation = 2 ** number
            gradients.append(lax.dot_general(gather_taps(levels[number], dilation), signal.reshape(height * width_all, channels), (((0,), (0,)), ((), ())), preferred_element_type=jnp.float32))
            backward = jnp.dot(gather_taps(signal, dilation), flipped[number], preferred_element_type=jnp.float32).reshape(height, width_all, channels)
            if number > 0:
                signal = (backward * slope(preacts[number - 1])).astype(jnp.bfloat16)
            else:
                input_grad = backward.astype(jnp.bfloat16)
        gradients = jnp.stack(gradients[::-1])
        return (totals + gradients, (levels[-1], input_grad))
    totals, outputs = lax.scan(one_image, jnp.zeros((LAYERS, 9 * channels, channels), jnp.float32), (images, cotangent))
    scale = 1.0 / math.sqrt(BATCH * LAT * WIDTH)
    return (outputs[0], outputs[1], totals * scale)
```

```python
import functools
import math

import jax
import jax.numpy as jnp
from jax import lax
from jax.experimental import pallas as pl
from jax.experimental.pallas import tpu as pltpu
from jax.sharding import PartitionSpec as P

LAYERS = 4
PAD = 8
BF16 = jnp.bfloat16
F32 = jnp.float32
MESH = pl.DeviceIdType.MESH


def swapped(value):
    return jnp.swapaxes(value, 0, 1)


def kernel(
    ring, images_ref, weights_ref, cotangent_ref, features_ref, input_grad_ref, owned_ref, *scratch
):
    groups, ranks = ring
    (staged, upstream, columns_up, taps, forward_w, backward_w, shifter, slabs, out_a, out_b) = scratch[:10]
    levels = scratch[10:14]
    signals = scratch[14:18]
    slopes = scratch[18]
    send_b, recv_b, send_l, recv_l, local_sem = scratch[19:24]
    halo_send, halo_recv, batch_send, batch_recv, lon_send, lon_recv = scratch[24:30]

    lon = lax.axis_index("lon")
    batch = lax.axis_index("batch")
    right, left = lax.rem(lon + 1, groups), lax.rem(lon + groups - 1, groups)
    rows, width, channels = staged.shape

    fetch_images = pltpu.make_async_copy(images_ref, staged, local_sem.at[0])
    fetch_taps = pltpu.make_async_copy(weights_ref, taps, local_sem.at[1])
    fetch_upstream = pltpu.make_async_copy(cotangent_ref, upstream, local_sem.at[2])
    fetch_images.start()
    fetch_taps.start()
    fetch_upstream.start()

    barrier = pltpu.get_barrier_semaphore()

    @pl.loop(1, groups)
    def _(step):
        pl.semaphore_signal(
            barrier, inc=1, device_id={"lon": lax.rem(lon + step, groups)}, device_id_type=MESH
        )

    @pl.loop(1, ranks)
    def _(step):
        pl.semaphore_signal(
            barrier, inc=1, device_id={"batch": lax.rem(batch + step, ranks)}, device_id_type=MESH
        )

    def halo_copy(kind, number, side, place):
        dilation = 2**number
        buffer = (levels, signals)[kind][number]
        source = width + place if side == 0 else dilation + place
        target = place if side == 0 else dilation + width + place
        return pltpu.make_async_remote_copy(
            src_ref=buffer.at[1, source],
            dst_ref=buffer.at[1, target],
            send_sem=halo_send.at[kind, number, side, place],
            recv_sem=halo_recv.at[kind, number, side, place],
            device_id={"lon": right if side == 0 else left},
            device_id_type=MESH,
        )

    def send_column(kind, number, column):
        dilation = 2**number
        if column < dilation:
            halo_copy(kind, number, 1, column).start()
        if column >= width - dilation:
            halo_copy(kind, number, 0, column - (width - dilation)).start()

    def fill(buffer, dilation, slot, value):
        shifter[slot, pl.ds(PAD, rows), :] = value
        buffer[0, slot] = shifter[slot, pl.ds(PAD - dilation, rows), :].astype(BF16)
        buffer[2, slot] = shifter[slot, pl.ds(PAD + dilation, rows), :].astype(BF16)

    def receive(kind, number, side, place):
        dilation = 2**number
        buffer = (levels, signals)[kind][number]
        halo_copy(kind, number, side, place).wait_recv()
        slot = place if side == 0 else dilation + width + place
        fill(buffer, dilation, slot, buffer[1, slot].astype(F32))

    def build_forward(number):
        for span in range(4):
            for row in range(3):
                for side in range(2):
                    column = span - side
                    block = (
                        taps[number, 3 * row + column]
                        if 0 <= column < 3
                        else jnp.zeros((channels, channels), BF16)
                    )
                    forward_w[
                        number,
                        pl.ds((3 * span + row) * channels, channels),
                        pl.ds(side * channels, channels),
                    ] = block

    def build_backward(number):
        for span in range(4):
            for row in range(3):
                for side in range(2):
                    column = span - side
                    block = (
                        taps[number, 8 - (3 * row + column)]
                        if 0 <= column < 3
                        else jnp.zeros((channels, channels), BF16)
                    )
                    backward_w[
                        number,
                        pl.ds(side * channels, channels),
                        pl.ds((3 * span + row) * channels, channels),
                    ] = block

    def gathered(buffer, dilation, column):
        return jnp.concatenate(
            [buffer[row, column + span * dilation] for span in range(4) for row in range(3)], axis=-1
        )

    def pairs_of(dilation):
        firsts = [c for c in range(width) if (c // dilation) % 2 == 0]
        inner = [c for c in firsts if c >= dilation and c + 2 * dilation < width]
        edge = [c for c in firsts if c not in inner]
        return inner, edge

    def forward_pair(number, column):
        dilation = 2**number
        summed = jnp.dot(
            gathered(levels[number], dilation, column),
            forward_w[number],
            preferred_element_type=F32,
        )
        for side in range(2):
            here = column + side * dilation
            z = summed[:, side * channels : (side + 1) * channels]
            sigma = 0.5 * jnp.tanh(0.5 * z) + 0.5
            act = z * sigma
            slope = sigma + act - act * sigma
            if number + 1 < LAYERS:
                slopes[number, here] = slope
                following = levels[number + 1]
                reach = 2 ** (number + 1)
                following[1, reach + here] = act.astype(BF16)
                fill(following, reach, reach + here, act)
            else:
                slabs[here] = act.astype(BF16)
                signal = columns_up[here].astype(F32) * slope
                signals[number][1, dilation + here] = signal.astype(BF16)
                fill(signals[number], dilation, dilation + here, signal)

    def backward_pair(number, column):
        dilation = 2**number
        back = lax.dot_general(
            gathered(signals[number], dilation, column),
            backward_w[number],
            (((1,), (1,)), ((), ())),
            preferred_element_type=F32,
        )
        for side in range(2):
            here = column + side * dilation
            value = back[:, side * channels : (side + 1) * channels]
            if number > 0:
                reach = dilation // 2
                value = value * slopes[number - 1, here]
                signals[number - 1][1, reach + here] = value.astype(BF16)
                fill(signals[number - 1], reach, reach + here, value)
            else:
                slabs[here] = value.astype(BF16)

    def run_layer(kind, number, pair, then_kind, then_number):
        dilation = 2**number
        inner, edge = pairs_of(dilation)
        for column in inner:
            pair(number, column)
        lefts = [c for c in edge if c < dilation]
        rights = [c for c in edge if c + 2 * dilation >= width]
        both = [c for c in lefts if c in rights]
        order = []
        if both:
            order = [both[i : i + 2] for i in range(0, len(both), 2)]
        else:
            order = [lefts[i : i + 2] for i in range(0, len(lefts), 2)]
            order += [rights[i : i + 2] for i in range(0, len(rights), 2)]
        for group in order:
            for column in group:
                if column < dilation:
                    receive(kind, number, 0, column)
                if column + 2 * dilation >= width:
                    receive(kind, number, 1, column + 2 * dilation - width)
            for column in group:
                pair(number, column)
            if then_number is not None:
                for column in group:
                    for here in (column, column + dilation):
                        send_column(then_kind, then_number, here)

    def weight_grad(number):
        dilation = 2**number
        signal = signals[number]
        lhs = jnp.concatenate(
            [
                signal[1, (2 - j) * dilation : (2 - j) * dilation + width].reshape(rows * width, channels)
                for j in range(3)
            ],
            axis=-1,
        )
        rhs = jnp.concatenate(
            [
                levels[number][i, dilation : dilation + width].reshape(rows * width, channels)
                for i in range(3)
            ],
            axis=-1,
        )
        total = lax.dot_general(lhs, rhs, (((0,), (0,)), ((), ())), preferred_element_type=F32)
        block = channels // ranks
        total = total.astype(BF16)
        for j in range(3):
            for i in range(3):
                piece = total[j * channels : (j + 1) * channels, i * channels : (i + 1) * channels]
                send_b[number, :, pl.ds((3 * i + j) * block, block), :] = piece.reshape(
                    ranks, block, channels
                )

    def batch_copy(number, step):
        target = lax.rem(batch + step, ranks)
        return pltpu.make_async_remote_copy(
            src_ref=send_b.at[number, target],
            dst_ref=recv_b.at[number, step],
            send_sem=batch_send.at[number, step],
            recv_sem=batch_recv.at[number, step],
            device_id={"batch": target},
            device_id_type=MESH,
        )

    def lon_copy(number, step):
        target = lax.rem(lon + step, groups)
        return pltpu.make_async_remote_copy(
            src_ref=send_l.at[number, target],
            dst_ref=recv_l.at[number, step],
            send_sem=lon_send.at[number, step],
            recv_sem=lon_recv.at[number, step],
            device_id={"lon": target},
            device_id_type=MESH,
        )

    def start_batch(number):
        @pl.loop(1, ranks)
        def _(step):
            batch_copy(number, step).start()

    def start_lon(number):
        @pl.loop(1, ranks)
        def _(step):
            batch_copy(number, step).wait_recv()

        total = send_b[number, batch].astype(F32)
        for step in range(1, ranks):
            total = total + recv_b[number, step].astype(F32)
        block = channels // ranks
        share = 9 * channels // groups
        lane = lax.broadcasted_iota(jnp.int32, (block, channels), 1)
        for target in range(groups):
            tap, offset = divmod(target * share, channels)
            value = total[tap * block : (tap + 1) * block]
            if offset:
                value = pltpu.roll(value, channels - offset, 1)
            if offset + share > channels:
                more = total[(tap + 1) * block : (tap + 2) * block]
                more = pltpu.roll(more, channels - offset, 1)
                value = jnp.where(lane < channels - offset, value, more)
            send_l[number, target] = value.astype(BF16)

        @pl.loop(1, groups)
        def _(step):
            lon_copy(number, step).start()

    def finish(number):
        @pl.loop(1, groups)
        def _(step):
            lon_copy(number, step).wait_recv()

        total = send_l[number, lon].astype(F32)
        for step in range(1, groups):
            total = total + recv_l[number, step].astype(F32)
        owned_ref[number] = total * (1.0 / math.sqrt(rows * width * groups * ranks))

    fetch_images.wait()
    level = levels[0]
    level[1, 1 : 1 + width] = swapped(staged[...])
    pl.semaphore_wait(barrier, groups + ranks - 2)
    send_column(0, 0, 0)
    send_column(0, 0, width - 1)
    edge_rows = jnp.zeros((PAD, channels), F32)
    for slot in range(shifter.shape[0]):
        shifter[slot, pl.ds(0, PAD), :] = edge_rows
        shifter[slot, pl.ds(PAD + rows, PAD), :] = edge_rows
    for column in range(width):
        fill(level, 1, 1 + column, level[1, 1 + column].astype(F32))
    fetch_taps.wait()
    build_forward(0)
    for number in range(LAYERS):
        if number + 1 < LAYERS:
            run_layer(0, number, forward_pair, 0, number + 1)
            build_forward(number + 1)
            if number == 0:
                fetch_upstream.wait()
                columns_up[...] = swapped(upstream[...])
        else:
            run_layer(0, number, forward_pair, 1, number)

    out_a[...] = swapped(slabs[...])
    store_features = pltpu.make_async_copy(out_a, features_ref, local_sem.at[3])
    store_features.start()
    for number in range(LAYERS):
        build_backward(number)
    for number in reversed(range(1, LAYERS)):
        run_layer(1, number, backward_pair, 1, number - 1)
        weight_grad(number)
        start_batch(number)
    start_lon(3)
    start_lon(2)
    receive(1, 0, 0, 0)
    receive(1, 0, 1, 0)
    weight_grad(0)
    start_batch(0)
    for column in range(0, width, 2):
        backward_pair(0, column)
    out_b[...] = swapped(slabs[...])
    store_grad = pltpu.make_async_copy(out_b, input_grad_ref, local_sem.at[4])
    store_grad.start()
    start_lon(1)
    start_lon(0)
    for number in reversed(range(LAYERS)):
        finish(number)

    for number in range(LAYERS):
        for kind in range(2):
            for side in range(2):
                for place in range(2**number):
                    halo_copy(kind, number, side, place).wait_send()

        @pl.loop(1, ranks)
        def _(step):
            batch_copy(number, step).wait_send()

        @pl.loop(1, groups)
        def _(step):
            lon_copy(number, step).wait_send()

    store_features.wait()
    store_grad.wait()


def local(images, weights, cotangent):
    _, rows, width, channels = images.shape
    groups, ranks = lax.axis_size("lon"), lax.axis_size("batch")
    block = channels // ranks
    field = (rows, width, channels)
    columns = (width, rows, channels)
    dilations = [2**number for number in range(LAYERS)]
    padded = [pltpu.VMEM((3, width + 2 * r, rows, channels), BF16) for r in dilations]
    features, input_grad, owned = pl.pallas_call(
        functools.partial(kernel, (groups, ranks)),
        out_shape=(
            jax.ShapeDtypeStruct(field, BF16),
            jax.ShapeDtypeStruct(field, BF16),
            jax.ShapeDtypeStruct((LAYERS, block, channels), F32),
        ),
        in_specs=[pl.BlockSpec(memory_space=pl.ANY)] * 3,
        out_specs=(
            pl.BlockSpec(memory_space=pl.ANY),
            pl.BlockSpec(memory_space=pl.ANY),
            pl.BlockSpec(memory_space=pltpu.VMEM),
        ),
        scratch_shapes=[
            pltpu.VMEM(field, BF16),
            pltpu.VMEM(field, BF16),
            pltpu.VMEM(columns, BF16),
            pltpu.VMEM((LAYERS, 9, channels, channels), BF16),
            pltpu.VMEM((LAYERS, 12 * channels, 2 * channels), BF16),
            pltpu.VMEM((LAYERS, 2 * channels, 12 * channels), BF16),
            pltpu.VMEM((width + 2 * dilations[-1], rows + 2 * PAD, channels), F32),
            pltpu.VMEM(columns, BF16),
            pltpu.VMEM(field, BF16),
            pltpu.VMEM(field, BF16),
            *padded,
            *padded,
            pltpu.VMEM((LAYERS - 1, *columns), F32),
            pltpu.VMEM((LAYERS, ranks, 9 * block, channels), BF16),
            pltpu.VMEM((LAYERS, ranks, 9 * block, channels), BF16),
            pltpu.VMEM((LAYERS, groups, block, channels), BF16),
            pltpu.VMEM((LAYERS, groups, block, channels), BF16),
            pltpu.SemaphoreType.DMA((5,)),
            pltpu.SemaphoreType.DMA((2, LAYERS, 2, dilations[-1])),
            pltpu.SemaphoreType.DMA((2, LAYERS, 2, dilations[-1])),
            pltpu.SemaphoreType.DMA((LAYERS, ranks)),
            pltpu.SemaphoreType.DMA((LAYERS, ranks)),
            pltpu.SemaphoreType.DMA((LAYERS, groups)),
            pltpu.SemaphoreType.DMA((LAYERS, groups)),
        ],
        compiler_params=pltpu.CompilerParams(
            collective_id=0, has_side_effects=True, vmem_limit_bytes=58 * 2**20
        ),
        name="panorama",
    )(images.reshape(field), weights, cotangent.reshape(field))
    share = 9 * channels // groups
    weight_grads = jnp.swapaxes(owned[:, :, :share], 1, 2)
    return features.reshape(images.shape), input_grad.reshape(images.shape), weight_grads


def solution(mesh):
    return jax.shard_map(
        local,
        mesh=mesh,
        in_specs=(P("batch", None, "lon", None), P(), P("batch", None, "lon", None)),
        out_specs=(
            P("batch", None, "lon", None),
            P("batch", None, "lon", None),
            P(None, "lon", "batch"),
        ),
        check_vma=False,
    )
```

```python
import functools
import math

import jax
import jax.numpy as jnp
from jax import lax
from jax.experimental import pallas as pl
from jax.experimental.pallas import tpu as pltpu
from jax.sharding import PartitionSpec as P

LAYERS = 4
PAD = 8
BF16 = jnp.bfloat16
F32 = jnp.float32
MESH = pl.DeviceIdType.MESH

LEVEL_PAD = (7, 6, 4, 8)
SIGNAL_PAD = (1, 2, 6, 8)
SLOPE_PAD = (0, 2, 0)
PIECES = (
    (((0, 1), (1, 2), (3, 2), (5, 2)), ((15, 1), (13, 2), (11, 2), (9, 2))),
    (((0, 2), (4, 2), (2, 2), (6, 2)), ((8, 2), (12, 2), (10, 2), (14, 2))),
    (((0, 2), (4, 2), (2, 2), (6, 2)), ((8, 2), (12, 2), (10, 2), (14, 2))),
    (((0, 2), (4, 2), (2, 2)), ((12, 2), (10, 2), (14, 2))),
    (((0, 1),), ((15, 1),)),
)


def swapped(value):
    return jnp.swapaxes(value, 0, 1)


def kernel(
    ring, images_ref, weights_ref, cotangent_ref, features_ref, input_grad_ref, owned_ref, *scratch
):
    groups, ranks = ring
    (staged, upstream, columns_up, taps, forward_w, backward_w, shifter, slabs) = scratch[:8]
    levels = scratch[8:12]
    signals = scratch[12:16]
    slopes = scratch[16:19]
    send_b, recv_b, send_l, recv_l, send_m, recv_m, local_sem = scratch[19:26]
    halo_send, halo_recv, batch_send, batch_recv, lon_send, lon_recv = scratch[26:32]

    lon = lax.axis_index("lon")
    batch = lax.axis_index("batch")
    right, left = lax.rem(lon + 1, groups), lax.rem(lon + groups - 1, groups)
    rows, width, channels = staged.shape
    block = channels // ranks
    share = 9 * channels // groups

    fetch_images = pltpu.make_async_copy(images_ref, staged, local_sem.at[0])
    fetch_taps = pltpu.make_async_copy(weights_ref, taps, local_sem.at[1])
    fetch_upstream = pltpu.make_async_copy(cotangent_ref, upstream, local_sem.at[2])
    fetch_images.start()
    fetch_taps.start()
    fetch_upstream.start()

    barrier = pltpu.get_barrier_semaphore()

    @pl.loop(1, groups)
    def _(step):
        pl.semaphore_signal(
            barrier, inc=1, device_id={"lon": lax.rem(lon + step, groups)}, device_id_type=MESH
        )

    @pl.loop(1, ranks)
    def _(step):
        pl.semaphore_signal(
            barrier, inc=1, device_id={"batch": lax.rem(batch + step, ranks)}, device_id_type=MESH
        )

    exchanged = (
        (levels[0], LEVEL_PAD[0]),
        (levels[3], LEVEL_PAD[3]),
        (signals[3], SIGNAL_PAD[3]),
        (signals[2], SIGNAL_PAD[2]),
        (signals[0], SIGNAL_PAD[0]),
    )

    def halo_copy(which, side, piece):
        buffer, pad = exchanged[which]
        first, count = PIECES[which][side][piece]
        landing = first + width if side == 0 else first - width
        return pltpu.make_async_remote_copy(
            src_ref=buffer.at[1, pad + first : pad + first + count],
            dst_ref=buffer.at[1, pad + landing : pad + landing + count],
            send_sem=halo_send.at[which, side, piece],
            recv_sem=halo_recv.at[which, side, piece],
            device_id={"lon": left if side == 0 else right},
            device_id_type=MESH,
        )

    def fill(buffer, dilation, slot, value):
        shifter[slot, pl.ds(PAD, rows), :] = value
        buffer[0, slot] = shifter[slot, pl.ds(PAD - dilation, rows), :].astype(BF16)
        buffer[2, slot] = shifter[slot, pl.ds(PAD + dilation, rows), :].astype(BF16)

    def receive(which, side, piece, dilation):
        buffer, pad = exchanged[which]
        halo_copy(which, side, piece).wait_recv()
        first, count = PIECES[which][side][piece]
        landing = pad + (first + width if side == 0 else first - width)
        for slot in range(landing, landing + count):
            fill(buffer, dilation, slot, buffer[1, slot].astype(F32))

    def tap_block(number, tap_row, tap_column, turned):
        if not 0 <= tap_column < 3:
            return jnp.zeros((channels, channels), BF16)
        tap = 3 * tap_row + tap_column
        return taps[number, 8 - tap if turned else tap]

    def build_forward(number):
        for span in range(4):
            for row in range(3):
                for side in range(2):
                    forward_w[
                        number,
                        pl.ds((3 * span + row) * channels, channels),
                        pl.ds(side * channels, channels),
                    ] = tap_block(number, row, span - side, False)

    def build_backward(number):
        for span in range(4):
            for row in range(3):
                for side in range(2):
                    backward_w[
                        number,
                        pl.ds(side * channels, channels),
                        pl.ds((3 * span + row) * channels, channels),
                    ] = tap_block(number, row, span - side, True)

    def gathered(buffer, pad, dilation, column, spans=4):
        return jnp.concatenate(
            [
                buffer[row, pad + column + (span - 1) * dilation]
                for span in range(spans)
                for row in range(3)
            ],
            axis=-1,
        )

    def forward_pair(number, column):
        dilation = 2**number
        summed = jnp.dot(
            gathered(levels[number], LEVEL_PAD[number], dilation, column),
            forward_w[number],
            preferred_element_type=F32,
        )
        for side in range(2):
            here = column + side * dilation
            z = summed[:, side * channels : (side + 1) * channels]
            sigma = 0.5 * jnp.tanh(0.5 * z) + 0.5
            act = z * sigma
            if number + 1 < LAYERS:
                if -SLOPE_PAD[number] <= here < width + SLOPE_PAD[number]:
                    slopes[number][SLOPE_PAD[number] + here] = sigma + act - act * sigma
                following, slot = levels[number + 1], LEVEL_PAD[number + 1] + here
                following[1, slot] = act.astype(BF16)
                fill(following, 2 * dilation, slot, act)
            else:
                slabs[here] = act.astype(BF16)
                signal = columns_up[here].astype(F32) * (sigma + act - act * sigma)
                slot = SIGNAL_PAD[number] + here
                signals[number][1, slot] = signal.astype(BF16)
                fill(signals[number], dilation, slot, signal)

    def backward_columns(number, column, sides):
        dilation = 2**number
        spans = 2 + sides
        back = lax.dot_general(
            gathered(signals[number], SIGNAL_PAD[number], dilation, column, spans),
            backward_w[number, pl.ds(0, sides * channels), pl.ds(0, 3 * spans * channels)],
            (((1,), (1,)), ((), ())),
            preferred_element_type=F32,
        )
        for side in range(sides):
            here = column + side * dilation
            value = back[:, side * channels : (side + 1) * channels]
            if number > 0:
                value = value * slopes[number - 1][SLOPE_PAD[number - 1] + here]
                slot = SIGNAL_PAD[number - 1] + here
                signals[number - 1][1, slot] = value.astype(BF16)
                fill(signals[number - 1], dilation // 2, slot, value)
            else:
                slabs[here] = value.astype(BF16)

    def weight_grad(number):
        dilation = 2**number
        signal, pad, level_pad = signals[number], SIGNAL_PAD[number], LEVEL_PAD[number]
        lhs = jnp.concatenate(
            [
                signal[1, pad + (1 - j) * dilation : pad + (1 - j) * dilation + width].reshape(
                    rows * width, channels
                )
                for j in range(3)
            ],
            axis=-1,
        )
        rhs = jnp.concatenate(
            [
                levels[number][i, level_pad : level_pad + width].reshape(rows * width, channels)
                for i in range(3)
            ],
            axis=-1,
        )
        total = lax.dot_general(lhs, rhs, (((0,), (0,)), ((), ())), preferred_element_type=F32)
        total = total.astype(BF16)
        for j in range(3):
            for i in range(3):
                piece = total[j * channels : (j + 1) * channels, i * channels : (i + 1) * channels]
                send_b[number, :, pl.ds((3 * i + j) * block, block), :] = piece.reshape(
                    ranks, block, channels
                )

    def batch_copy(number, step):
        target = lax.rem(batch + step, ranks)
        return pltpu.make_async_remote_copy(
            src_ref=send_b.at[number, target],
            dst_ref=recv_b.at[number, step],
            send_sem=batch_send.at[number, step],
            recv_sem=batch_recv.at[number, step],
            device_id={"batch": target},
            device_id_type=MESH,
        )

    sets = ((send_l, recv_l, (0,)), (send_m, recv_m, (3, 2, 1)))

    def lon_copy(which, step):
        source, landing, _ = sets[which]
        target = lax.rem(lon + step, groups)
        return pltpu.make_async_remote_copy(
            src_ref=source.at[target],
            dst_ref=landing.at[step],
            send_sem=lon_send.at[which, step],
            recv_sem=lon_recv.at[which, step],
            device_id={"lon": target},
            device_id_type=MESH,
        )

    def start_batch(number):
        @pl.loop(1, ranks)
        def _(step):
            batch_copy(number, step).start()

    lane = lax.broadcasted_iota(jnp.int32, (block, channels), 1)

    def prepare_lon(which):
        source, _, numbers = sets[which]
        for place, number in enumerate(numbers):

            @pl.loop(1, ranks)
            def _(step):
                batch_copy(number, step).wait_recv()

            total = send_b[number, batch].astype(F32)
            for step in range(1, ranks):
                total = total + recv_b[number, step].astype(F32)
            for target in range(groups):
                tap, offset = divmod(target * share, channels)
                value = total[tap * block : (tap + 1) * block]
                if offset:
                    value = pltpu.roll(value, channels - offset, 1)
                if offset + share > channels:
                    more = total[(tap + 1) * block : (tap + 2) * block]
                    more = pltpu.roll(more, channels - offset, 1)
                    value = jnp.where(lane < channels - offset, value, more)
                source[target, pl.ds(place * block, block), :] = value.astype(BF16)

    def start_lon(which):
        prepare_lon(which)

        @pl.loop(1, groups)
        def _(step):
            lon_copy(which, step).start()

    def finish(which):
        @pl.loop(1, groups)
        def _(step):
            lon_copy(which, step).wait_recv()

        source, landing, numbers = sets[which]
        total = source[lon].astype(F32)
        for step in range(1, groups):
            total = total + landing[step].astype(F32)
        total = total * (1.0 / math.sqrt(rows * width * groups * ranks))
        for place, number in enumerate(numbers):
            owned_ref[number] = total[place * block : (place + 1) * block, :share]

    fetch_images.wait()
    level, pad = levels[0], LEVEL_PAD[0]
    level[1, pad : pad + width] = swapped(staged[...])
    pl.semaphore_wait(barrier, groups + ranks - 2)
    for piece in range(4):
        for side in range(2):
            halo_copy(0, side, piece).start()
    edge_rows = jnp.zeros((PAD, channels), F32)
    for slot in range(shifter.shape[0]):
        shifter[slot, pl.ds(0, PAD), :] = edge_rows
        shifter[slot, pl.ds(PAD + rows, PAD), :] = edge_rows
    for column in range(width):
        fill(level, 1, pad + column, level[1, pad + column].astype(F32))
    fetch_taps.wait()
    build_forward(0)
    for column in range(2, width - 2, 2):
        forward_pair(0, column)
    build_forward(1)
    for column in (4, 5, 8, 9):
        forward_pair(1, column)
    fetch_upstream.wait()
    columns_up[...] = swapped(upstream[...])
    for number in (2, 3):
        build_forward(number)
    for piece in range(4):
        receive(0, 0, piece, 1)
        receive(0, 1, piece, 1)
        forward_pair(0, -2 * piece)
        forward_pair(0, width - 2 + 2 * piece)
        if piece == 1:
            for column in (0, 1, 12, 13):
                forward_pair(1, column)
    for column in (-4, -3, 16, 17):
        forward_pair(1, column)
    for first in (0, 2):
        for side in range(2):
            for column in (first, first + 1):
                forward_pair(2, column + 8 * side)
            halo_copy(1, side, first).start()
            halo_copy(1, side, first + 1).start()
    for number in range(LAYERS):
        build_backward(number)
    for piece, first in enumerate((0, 4, 2, 6)):
        receive(1, 0, piece, 8)
        receive(1, 1, piece, 8)
        forward_pair(3, first)
        forward_pair(3, first + 1)
        halo_copy(2, 0, piece).start()
        halo_copy(2, 1, piece).start()

    features_ref[...] = swapped(slabs[...])
    ready = (((0, 0),), ((0, 1), (1, 0)), ((0, 2), (1, 1)), ((1, 2),))
    for piece, first in enumerate((0, 4, 2, 6)):
        receive(2, 0, piece, 8)
        receive(2, 1, piece, 8)
        backward_columns(3, first, 2)
        backward_columns(3, first + 1, 2)
        for side, part in ready[piece]:
            halo_copy(3, side, part).start()
    weight_grad(3)
    start_batch(3)
    for side in range(2):
        for piece in range(3):
            receive(3, side, piece, 4)
    for column in (0, 1, 2, 3, 8, 9, 10, 11):
        backward_columns(2, column, 2)
    for column in (-2, -1, 16, 17):
        backward_columns(2, column, 1)
    for column in (0, 13):
        backward_columns(1, column, 2)
    halo_copy(4, 0, 0).start()
    halo_copy(4, 1, 0).start()
    for column in (1, 4, 5, 8, 9, 12):
        backward_columns(1, column, 2)
    weight_grad(2)
    start_batch(2)
    weight_grad(1)
    start_batch(1)
    receive(4, 0, 0, 1)
    receive(4, 1, 0, 1)
    weight_grad(0)
    start_batch(0)
    for column in range(0, width, 2):
        backward_columns(0, column, 2)
    input_grad_ref[...] = swapped(slabs[...])
    start_lon(1)
    start_lon(0)
    finish(1)
    finish(0)

    for which in range(len(PIECES)):
        for side in range(2):
            for piece in range(len(PIECES[which][side])):
                halo_copy(which, side, piece).wait_send()
    for number in range(LAYERS):

        @pl.loop(1, ranks)
        def _(step):
            batch_copy(number, step).wait_send()

    for which in range(2):

        @pl.loop(1, groups)
        def _(step):
            lon_copy(which, step).wait_send()


def local(images, weights, cotangent):
    _, rows, width, channels = images.shape
    groups, ranks = lax.axis_size("lon"), lax.axis_size("batch")
    block = channels // ranks
    share = 9 * channels // groups
    field = (rows, width, channels)

    def columns(pad, *front):
        return (*front, width + 2 * pad, rows, channels)

    features, input_grad, owned = pl.pallas_call(
        functools.partial(kernel, (groups, ranks)),
        out_shape=(
            pltpu.VMEM(field, BF16),
            pltpu.VMEM(field, BF16),
            pltpu.VMEM((LAYERS, block, share), F32),
        ),
        in_specs=[pl.BlockSpec(memory_space=pl.ANY)] * 3,
        out_specs=(pl.BlockSpec(memory_space=pltpu.VMEM),) * 3,
        scratch_shapes=[
            pltpu.VMEM(field, BF16),
            pltpu.VMEM(field, BF16),
            pltpu.VMEM(columns(0), BF16),
            pltpu.VMEM((LAYERS, 9, channels, channels), BF16),
            pltpu.VMEM((LAYERS, 12 * channels, 2 * channels), BF16),
            pltpu.VMEM((LAYERS, 2 * channels, 12 * channels), BF16),
            pltpu.VMEM((width + 2 * max(LEVEL_PAD), rows + 2 * PAD, channels), F32),
            pltpu.VMEM(columns(0), BF16),
            *[pltpu.VMEM(columns(pad, 3), BF16) for pad in LEVEL_PAD],
            *[pltpu.VMEM(columns(pad, 3), BF16) for pad in SIGNAL_PAD],
            *[pltpu.VMEM(columns(pad), F32) for pad in SLOPE_PAD],
            pltpu.VMEM((LAYERS, ranks, 9 * block, channels), BF16),
            pltpu.VMEM((LAYERS, ranks, 9 * block, channels), BF16),
            pltpu.VMEM((groups, block, channels), BF16),
            pltpu.VMEM((groups, block, channels), BF16),
            pltpu.VMEM((groups, 3 * block, channels), BF16),
            pltpu.VMEM((groups, 3 * block, channels), BF16),
            pltpu.SemaphoreType.DMA((3,)),
            pltpu.SemaphoreType.DMA((len(PIECES), 2, 4)),
            pltpu.SemaphoreType.DMA((len(PIECES), 2, 4)),
            pltpu.SemaphoreType.DMA((LAYERS, ranks)),
            pltpu.SemaphoreType.DMA((LAYERS, ranks)),
            pltpu.SemaphoreType.DMA((2, groups)),
            pltpu.SemaphoreType.DMA((2, groups)),
        ],
        compiler_params=pltpu.CompilerParams(
            collective_id=0, has_side_effects=True, vmem_limit_bytes=58 * 2**20
        ),
        name="panorama",
    )(images.reshape(field), weights, cotangent.reshape(field))
    weight_grads = jnp.swapaxes(owned, 1, 2)
    return features.reshape(images.shape), input_grad.reshape(images.shape), weight_grads


def solution(mesh):
    return jax.shard_map(
        local,
        mesh=mesh,
        in_specs=(P("batch", None, "lon", None), P(), P("batch", None, "lon", None)),
        out_specs=(
            P("batch", None, "lon", None),
            P("batch", None, "lon", None),
            P(None, "lon", "batch"),
        ),
        check_vma=False,
    )
```

```python
import functools
import math

import jax
import jax.numpy as jnp
from jax import lax
from jax.experimental import pallas as pl
from jax.experimental.pallas import tpu as pltpu
from jax.sharding import PartitionSpec as P

LAYERS = 4
PAD = 8
BF16 = jnp.bfloat16
F32 = jnp.float32
MESH = pl.DeviceIdType.MESH

LEVEL_PAD = (7, 6, 4, 8)
SIGNAL_PAD = (1, 2, 6, 8)
SLOPE_PAD = (0, 2, 0)
PIECES = (
    (((0, 1), (1, 2), (3, 2), (5, 2)), ((15, 1), (13, 2), (11, 2), (9, 2))),
    (((0, 2), (4, 2), (2, 2), (6, 2)), ((8, 2), (12, 2), (10, 2), (14, 2))),
    (((0, 2), (4, 2), (2, 2), (6, 2)), ((8, 2), (12, 2), (10, 2), (14, 2))),
    (((0, 2), (4, 2), (2, 2)), ((12, 2), (10, 2), (14, 2))),
    (((0, 1),), ((15, 1),)),
)


def swapped(value):
    return jnp.swapaxes(value, 0, 1)


def kernel(
    ring, images_ref, weights_ref, cotangent_ref, features_ref, input_grad_ref, owned_ref, *scratch
):
    groups, ranks = ring
    (staged, upstream, columns_up, taps, forward_w, backward_w, shifter, slabs) = scratch[:8]
    levels = scratch[8:12]
    signals = scratch[12:16]
    slopes = scratch[16:19]
    send_b, recv_b, send_l, recv_l, local_sem = scratch[19:24]
    halo_send, halo_recv, batch_send, batch_recv, lon_send, lon_recv = scratch[24:30]

    lon = lax.axis_index("lon")
    batch = lax.axis_index("batch")
    right, left = lax.rem(lon + 1, groups), lax.rem(lon + groups - 1, groups)
    rows, width, channels = staged.shape
    block = channels // ranks
    share = 9 * channels // groups

    fetch_images = pltpu.make_async_copy(images_ref, staged, local_sem.at[0])
    fetch_taps = pltpu.make_async_copy(weights_ref, taps, local_sem.at[1])
    fetch_upstream = pltpu.make_async_copy(cotangent_ref, upstream, local_sem.at[2])
    fetch_images.start()
    fetch_taps.start()
    fetch_upstream.start()

    barrier = pltpu.get_barrier_semaphore()

    @pl.loop(1, groups)
    def _(step):
        pl.semaphore_signal(
            barrier, inc=1, device_id={"lon": lax.rem(lon + step, groups)}, device_id_type=MESH
        )

    @pl.loop(1, ranks)
    def _(step):
        pl.semaphore_signal(
            barrier, inc=1, device_id={"batch": lax.rem(batch + step, ranks)}, device_id_type=MESH
        )

    exchanged = (
        (levels[0], LEVEL_PAD[0]),
        (levels[3], LEVEL_PAD[3]),
        (signals[3], SIGNAL_PAD[3]),
        (signals[2], SIGNAL_PAD[2]),
        (signals[0], SIGNAL_PAD[0]),
    )

    def halo_copy(which, side, piece):
        buffer, pad = exchanged[which]
        first, count = PIECES[which][side][piece]
        landing = first + width if side == 0 else first - width
        return pltpu.make_async_remote_copy(
            src_ref=buffer.at[1, pad + first : pad + first + count],
            dst_ref=buffer.at[1, pad + landing : pad + landing + count],
            send_sem=halo_send.at[which, side, piece],
            recv_sem=halo_recv.at[which, side, piece],
            device_id={"lon": left if side == 0 else right},
            device_id_type=MESH,
        )

    def fill(buffer, dilation, slot, value):
        shifter[slot, pl.ds(PAD, rows), :] = value
        buffer[0, slot] = shifter[slot, pl.ds(PAD - dilation, rows), :].astype(BF16)
        buffer[2, slot] = shifter[slot, pl.ds(PAD + dilation, rows), :].astype(BF16)

    def receive(which, side, piece, dilation):
        buffer, pad = exchanged[which]
        halo_copy(which, side, piece).wait_recv()
        first, count = PIECES[which][side][piece]
        landing = pad + (first + width if side == 0 else first - width)
        for slot in range(landing, landing + count):
            fill(buffer, dilation, slot, buffer[1, slot].astype(F32))

    def tap_block(number, tap_row, tap_column, turned):
        if not 0 <= tap_column < 3:
            return jnp.zeros((channels, channels), BF16)
        tap = 3 * tap_row + tap_column
        return taps[number, 8 - tap if turned else tap]

    def build_forward(number):
        for span in range(4):
            for row in range(3):
                for side in range(2):
                    forward_w[
                        number,
                        pl.ds((3 * span + row) * channels, channels),
                        pl.ds(side * channels, channels),
                    ] = tap_block(number, row, span - side, False)

    def build_backward(number):
        for span in range(4):
            for row in range(3):
                for side in range(2):
                    backward_w[
                        number,
                        pl.ds(side * channels, channels),
                        pl.ds((3 * span + row) * channels, channels),
                    ] = tap_block(number, row, span - side, True)

    def gathered(buffer, pad, dilation, column, spans=4):
        return jnp.concatenate(
            [
                buffer[row, pad + column + (span - 1) * dilation]
                for span in range(spans)
                for row in range(3)
            ],
            axis=-1,
        )

    def forward_pair(number, column):
        dilation = 2**number
        summed = jnp.dot(
            gathered(levels[number], LEVEL_PAD[number], dilation, column),
            forward_w[number],
            preferred_element_type=F32,
        )
        for side in range(2):
            here = column + side * dilation
            z = summed[:, side * channels : (side + 1) * channels]
            sigma = 0.5 * jnp.tanh(0.5 * z) + 0.5
            act = z * sigma
            if number + 1 < LAYERS:
                if -SLOPE_PAD[number] <= here < width + SLOPE_PAD[number]:
                    slopes[number][SLOPE_PAD[number] + here] = sigma + act - act * sigma
                following, slot = levels[number + 1], LEVEL_PAD[number + 1] + here
                following[1, slot] = act.astype(BF16)
                fill(following, 2 * dilation, slot, act)
            else:
                slabs[here] = act.astype(BF16)
                signal = columns_up[here].astype(F32) * (sigma + act - act * sigma)
                slot = SIGNAL_PAD[number] + here
                signals[number][1, slot] = signal.astype(BF16)
                fill(signals[number], dilation, slot, signal)

    def backward_columns(number, column, sides):
        dilation = 2**number
        spans = 2 + sides
        back = lax.dot_general(
            gathered(signals[number], SIGNAL_PAD[number], dilation, column, spans),
            backward_w[number, pl.ds(0, sides * channels), pl.ds(0, 3 * spans * channels)],
            (((1,), (1,)), ((), ())),
            preferred_element_type=F32,
        )
        for side in range(sides):
            here = column + side * dilation
            value = back[:, side * channels : (side + 1) * channels]
            if number > 0:
                value = value * slopes[number - 1][SLOPE_PAD[number - 1] + here]
                slot = SIGNAL_PAD[number - 1] + here
                signals[number - 1][1, slot] = value.astype(BF16)
                fill(signals[number - 1], dilation // 2, slot, value)
            else:
                slabs[here] = value.astype(BF16)

    def weight_grad(number):
        dilation = 2**number
        pad, level_pad = SIGNAL_PAD[number], LEVEL_PAD[number]
        signal = signals[number][1, pad : pad + width].reshape(rows * width, channels)
        for j in range(3):
            first = level_pad + (j - 1) * dilation
            taken = jnp.concatenate(
                [
                    levels[number][i, first : first + width].reshape(rows * width, channels)
                    for i in range(3)
                ],
                axis=-1,
            )
            total = lax.dot_general(
                signal, taken, (((0,), (0,)), ((), ())), preferred_element_type=F32
            ).astype(BF16)
            for i in range(3):
                send_b[number, :, pl.ds((3 * i + j) * block, block), :] = total[
                    :, i * channels : (i + 1) * channels
                ].reshape(ranks, block, channels)

    def start_batch(number):
        half = ranks // 4
        for step in (half, 3 * half, *(n for n in range(1, ranks) if n not in (half, 3 * half))):
            target = lax.rem(batch + step, ranks)
            pltpu.make_async_remote_copy(
                src_ref=send_b.at[number, target],
                dst_ref=recv_b.at[number, step],
                send_sem=batch_send.at[number],
                recv_sem=batch_recv.at[number],
                device_id={"batch": target},
                device_id_type=MESH,
            ).start()

    sets = ((3, 2), (0, 1))

    lane = lax.broadcasted_iota(jnp.int32, (block, channels), 1)

    def start_lon(which):
        totals = []
        for number in sets[which]:
            arrived = recv_b.at[number, 1:]
            pltpu.make_async_copy(arrived, arrived, batch_recv.at[number]).wait()
            total = send_b[number, batch].astype(F32)
            for step in range(1, ranks):
                total = total + recv_b[number, step].astype(F32)
            totals.append(total)

        def shifted(total, tap, amount):
            value = total[tap * block : (tap + 1) * block]
            return pltpu.roll(value, amount, 1) if amount else value

        for target in range(groups):
            tap, offset = divmod(target * share, channels)
            packed = None
            for place, total in enumerate(totals):
                amount = (place * share - offset) % channels
                value = shifted(total, tap, amount)
                if offset + share > channels:
                    more = shifted(total, tap + 1, amount)
                    value = jnp.where(lane < place * share + channels - offset, value, more)
                packed = value if packed is None else jnp.where(lane < place * share, packed, value)
            send_l[which, target] = packed.astype(BF16)

        @pl.loop(0, groups - 1)
        def _(turn):
            rank = turn // 2
            apart = ((rank + 1) // 2) * (2 * (rank % 2) - 1)
            step = (groups // 4 + (turn % 2) * (groups // 2) + apart + groups) % groups
            target = lax.rem(lon + step, groups)
            pltpu.make_async_remote_copy(
                src_ref=send_l.at[which, target],
                dst_ref=recv_l.at[which, step],
                send_sem=lon_send.at[which],
                recv_sem=lon_recv.at[which],
                device_id={"lon": target},
                device_id_type=MESH,
            ).start()

    def finish(which):
        arrived = recv_l.at[which, 1:]
        pltpu.make_async_copy(arrived, arrived, lon_recv.at[which]).wait()
        total = send_l[which, lon].astype(F32)
        for step in range(1, groups):
            total = total + recv_l[which, step].astype(F32)
        total = total * (1.0 / math.sqrt(rows * width * groups * ranks))
        for place, number in enumerate(sets[which]):
            owned_ref[number] = total[:, place * share : (place + 1) * share]

    fetch_images.wait()
    level, pad = levels[0], LEVEL_PAD[0]
    level[1, pad : pad + width] = swapped(staged[...])
    pl.semaphore_wait(barrier, groups + ranks - 2)
    for piece in range(4):
        for side in range(2):
            halo_copy(0, side, piece).start()
    edge_rows = jnp.zeros((PAD, channels), F32)
    for slot in range(shifter.shape[0]):
        shifter[slot, pl.ds(0, PAD), :] = edge_rows
        shifter[slot, pl.ds(PAD + rows, PAD), :] = edge_rows
    for column in range(width):
        fill(level, 1, pad + column, level[1, pad + column].astype(F32))
    fetch_taps.wait()
    build_forward(0)
    for column in range(2, width - 2, 2):
        forward_pair(0, column)
    build_forward(1)
    for column in (4, 5, 8, 9):
        forward_pair(1, column)
    fetch_upstream.wait()
    columns_up[...] = swapped(upstream[...])
    for number in (2, 3):
        build_forward(number)
    for half in range(2):
        for piece in (2 * half, 2 * half + 1):
            receive(0, 0, piece, 1)
            receive(0, 1, piece, 1)
        for piece in (2 * half, 2 * half + 1):
            forward_pair(0, -2 * piece)
            forward_pair(0, width - 2 + 2 * piece)
        for column in ((0, 1, 12, 13), (-4, -3, 16, 17))[half]:
            forward_pair(1, column)
    for first in (0, 2):
        for side in range(2):
            for column in (first, first + 1):
                forward_pair(2, column + 8 * side)
            halo_copy(1, side, first).start()
            halo_copy(1, side, first + 1).start()
    for number in range(LAYERS):
        build_backward(number)
    for half, columns in enumerate(((0, 1, 4, 5), (2, 3, 6, 7))):
        for piece in (2 * half, 2 * half + 1):
            receive(1, 0, piece, 8)
            receive(1, 1, piece, 8)
        for place, column in enumerate(columns):
            forward_pair(3, column)
            if place % 2:
                halo_copy(2, 0, 2 * half + place // 2).start()
                halo_copy(2, 1, 2 * half + place // 2).start()

    features_ref[...] = swapped(slabs[...])
    ready = (((0, 0),), ((0, 1), (1, 0)), ((0, 2), (1, 1)), ((1, 2),))
    for half, columns in enumerate(((0, 1, 4, 5), (2, 3, 6, 7))):
        for piece in (2 * half, 2 * half + 1):
            receive(2, 0, piece, 8)
            receive(2, 1, piece, 8)
        for place, column in enumerate(columns):
            backward_columns(3, column, 2)
            if place % 2:
                for side, part in ready[2 * half + place // 2]:
                    halo_copy(3, side, part).start()
    weight_grad(3)
    start_batch(3)
    weight_grad(2)
    start_batch(2)
    for side in range(2):
        for piece in range(3):
            receive(3, side, piece, 4)
    for column in (0, 1, 2, 3, 8, 9, 10, 11):
        backward_columns(2, column, 2)
    for column in (-2, -1, 16, 17):
        backward_columns(2, column, 1)
    for column in (0, 13, 1, 4, 5, 8, 9, 12):
        backward_columns(1, column, 2)
        if column == 13:
            halo_copy(4, 0, 0).start()
            halo_copy(4, 1, 0).start()
    weight_grad(0)
    start_batch(0)
    weight_grad(1)
    start_batch(1)
    start_lon(0)
    receive(4, 0, 0, 1)
    receive(4, 1, 0, 1)
    for column in range(0, width, 2):
        backward_columns(0, column, 2)
    input_grad_ref[...] = swapped(slabs[...])
    start_lon(1)
    finish(0)
    finish(1)

    for which in range(len(PIECES)):
        for side in range(2):
            for piece in range(len(PIECES[which][side])):
                halo_copy(which, side, piece).wait_send()
    for number in range(LAYERS):
        sent = send_b.at[number, 1:]
        pltpu.make_async_copy(sent, sent, batch_send.at[number]).wait()
    for which in range(2):
        sent = send_l.at[which, 1:]
        pltpu.make_async_copy(sent, sent, lon_send.at[which]).wait()


def local(images, weights, cotangent):
    _, rows, width, channels = images.shape
    groups, ranks = lax.axis_size("lon"), lax.axis_size("batch")
    block = channels // ranks
    share = 9 * channels // groups
    field = (rows, width, channels)

    def columns(pad, *front):
        return (*front, width + 2 * pad, rows, channels)

    features, input_grad, owned = pl.pallas_call(
        functools.partial(kernel, (groups, ranks)),
        out_shape=(
            pltpu.VMEM(field, BF16),
            pltpu.VMEM(field, BF16),
            pltpu.VMEM((LAYERS, block, share), F32),
        ),
        in_specs=[pl.BlockSpec(memory_space=pl.ANY)] * 3,
        out_specs=(pl.BlockSpec(memory_space=pltpu.VMEM),) * 3,
        scratch_shapes=[
            pltpu.VMEM(field, BF16),
            pltpu.VMEM(field, BF16),
            pltpu.VMEM(columns(0), BF16),
            pltpu.VMEM((LAYERS, 9, channels, channels), BF16),
            pltpu.VMEM((LAYERS, 12 * channels, 2 * channels), BF16),
            pltpu.VMEM((LAYERS, 2 * channels, 12 * channels), BF16),
            pltpu.VMEM((width + 2 * max(LEVEL_PAD), rows + 2 * PAD, channels), F32),
            pltpu.VMEM(columns(0), BF16),
            *[pltpu.VMEM(columns(pad, 3), BF16) for pad in LEVEL_PAD],
            *[pltpu.VMEM(columns(pad, 3), BF16) for pad in SIGNAL_PAD],
            *[pltpu.VMEM(columns(pad), F32) for pad in SLOPE_PAD],
            pltpu.VMEM((LAYERS, ranks, 9 * block, channels), BF16),
            pltpu.VMEM((LAYERS, ranks, 9 * block, channels), BF16),
            pltpu.VMEM((2, groups, block, channels), BF16),
            pltpu.VMEM((2, groups, block, channels), BF16),
            pltpu.SemaphoreType.DMA((3,)),
            pltpu.SemaphoreType.DMA((len(PIECES), 2, 4)),
            pltpu.SemaphoreType.DMA((len(PIECES), 2, 4)),
            pltpu.SemaphoreType.DMA((LAYERS,)),
            pltpu.SemaphoreType.DMA((LAYERS,)),
            pltpu.SemaphoreType.DMA((2,)),
            pltpu.SemaphoreType.DMA((2,)),
        ],
        compiler_params=pltpu.CompilerParams(
            collective_id=0, has_side_effects=True, vmem_limit_bytes=58 * 2**20
        ),
        name="panorama",
    )(images.reshape(field), weights, cotangent.reshape(field))
    weight_grads = jnp.swapaxes(owned, 1, 2)
    return features.reshape(images.shape), input_grad.reshape(images.shape), weight_grads


def solution(mesh):
    return jax.shard_map(
        local,
        mesh=mesh,
        in_specs=(P("batch", None, "lon", None), P(), P("batch", None, "lon", None)),
        out_specs=(
            P("batch", None, "lon", None),
            P("batch", None, "lon", None),
            P(None, "lon", "batch"),
        ),
        check_vma=False,
    )
```

```python
import functools
import math

import jax
import jax.numpy as jnp
from jax import lax
from jax.experimental import pallas as pl
from jax.experimental.pallas import tpu as pltpu
from jax.sharding import PartitionSpec as P

LAYERS = 4
PAD = 8
BF16 = jnp.bfloat16
F32 = jnp.float32
MESH = pl.DeviceIdType.MESH

LEVEL_PAD = (7, 6, 4, 8)
SIGNAL_PAD = (1, 2, 6, 8)
SLOPE_PAD = (0, 2, 0)
PIECES = (
    (((0, 3), (3, 4)), ((13, 3), (9, 4))),
    (((0, 2), (4, 2), (2, 2), (6, 2)), ((8, 2), (12, 2), (10, 2), (14, 2))),
    (((0, 2), (4, 2), (2, 2), (6, 2)), ((8, 2), (12, 2), (10, 2), (14, 2))),
    (((0, 2), (4, 2), (2, 2)), ((12, 2), (10, 2), (14, 2))),
    (((0, 1),), ((15, 1),)),
)


def swapped(value):
    return jnp.swapaxes(value, 0, 1)


def kernel(
    ring, images_ref, weights_ref, cotangent_ref, features_ref, input_grad_ref, owned_ref, *scratch
):
    groups, ranks = ring
    (staged, upstream, columns_up, taps, forward_w, backward_w, shifter, slabs) = scratch[:8]
    levels = scratch[8:12]
    signals = scratch[12:16]
    slopes = scratch[16:19]
    send_b, recv_b, send_l, recv_l, partial, local_sem = scratch[19:25]
    halo_send, halo_recv, batch_send, batch_recv, lon_send, lon_recv = scratch[25:31]

    lon = lax.axis_index("lon")
    batch = lax.axis_index("batch")
    right, left = lax.rem(lon + 1, groups), lax.rem(lon + groups - 1, groups)
    rows, width, channels = staged.shape
    block = channels // ranks
    share = 9 * channels // groups

    fetch_images = pltpu.make_async_copy(images_ref, staged, local_sem.at[0])
    fetch_taps = pltpu.make_async_copy(weights_ref, taps, local_sem.at[1])
    fetch_upstream = pltpu.make_async_copy(cotangent_ref, upstream, local_sem.at[2])
    fetch_images.start()
    fetch_taps.start()
    fetch_upstream.start()

    barrier = pltpu.get_barrier_semaphore()

    @pl.loop(1, groups)
    def _(step):
        pl.semaphore_signal(
            barrier, inc=1, device_id={"lon": lax.rem(lon + step, groups)}, device_id_type=MESH
        )

    @pl.loop(1, ranks)
    def _(step):
        pl.semaphore_signal(
            barrier, inc=1, device_id={"batch": lax.rem(batch + step, ranks)}, device_id_type=MESH
        )

    exchanged = (
        (levels[0], LEVEL_PAD[0]),
        (levels[3], LEVEL_PAD[3]),
        (signals[3], SIGNAL_PAD[3]),
        (signals[2], SIGNAL_PAD[2]),
        (signals[0], SIGNAL_PAD[0]),
    )

    def halo_copy(which, side, piece):
        buffer, pad = exchanged[which]
        first, count = PIECES[which][side][piece]
        landing = first + width if side == 0 else first - width
        return pltpu.make_async_remote_copy(
            src_ref=buffer.at[1, pad + first : pad + first + count],
            dst_ref=buffer.at[1, pad + landing : pad + landing + count],
            send_sem=halo_send.at[which, side, piece],
            recv_sem=halo_recv.at[which, side, piece],
            device_id={"lon": left if side == 0 else right},
            device_id_type=MESH,
        )

    def fill(buffer, dilation, slot, value):
        shifter[slot, pl.ds(PAD, rows), :] = value
        buffer[0, slot] = shifter[slot, pl.ds(PAD - dilation, rows), :].astype(BF16)
        buffer[2, slot] = shifter[slot, pl.ds(PAD + dilation, rows), :].astype(BF16)

    def receive(which, side, piece, dilation):
        buffer, pad = exchanged[which]
        halo_copy(which, side, piece).wait_recv()
        first, count = PIECES[which][side][piece]
        landing = pad + (first + width if side == 0 else first - width)
        for slot in range(landing, landing + count):
            fill(buffer, dilation, slot, buffer[1, slot].astype(F32))

    def tap_block(number, tap_row, tap_column, turned):
        if not 0 <= tap_column < 3:
            return jnp.zeros((channels, channels), BF16)
        tap = 3 * tap_row + tap_column
        return taps[number, 8 - tap if turned else tap]

    def build_forward(number):
        for span in range(4):
            for row in range(3):
                for side in range(2):
                    forward_w[
                        number,
                        pl.ds((3 * span + row) * channels, channels),
                        pl.ds(side * channels, channels),
                    ] = tap_block(number, row, span - side, False)

    def build_backward(number):
        for span in range(4):
            for row in range(3):
                for side in range(2):
                    backward_w[
                        number,
                        pl.ds(side * channels, channels),
                        pl.ds((3 * span + row) * channels, channels),
                    ] = tap_block(number, row, span - side, True)

    def gathered(buffer, pad, dilation, column, spans=range(4)):
        return jnp.concatenate(
            [
                buffer[row, pad + column + (span - 1) * dilation]
                for span in spans
                for row in range(3)
            ],
            axis=-1,
        )

    inner, outer = (1, 2), (0, 3)
    third = 3 * channels

    def forward_part(number, column, spans):
        return jnp.dot(
            gathered(levels[number], LEVEL_PAD[number], 2**number, column, spans),
            jnp.concatenate([forward_w[number, pl.ds(span * third, third), :] for span in spans], axis=0),
            preferred_element_type=F32,
        )

    def backward_part(number, column, spans, sides=2):
        return lax.dot_general(
            gathered(signals[number], SIGNAL_PAD[number], 2**number, column, spans),
            jnp.concatenate(
                [
                    backward_w[number, pl.ds(0, sides * channels), pl.ds(span * third, third)]
                    for span in spans
                ],
                axis=1,
            ),
            (((1,), (1,)), ((), ())),
            preferred_element_type=F32,
        )

    def forward_pair(number, column):
        dilation = 2**number
        if number + 1 < LAYERS:
            summed = forward_part(number, column, range(4))
        else:
            summed = partial[column] + forward_part(number, column, outer)
        for side in range(2):
            here = column + side * dilation
            z = summed[:, side * channels : (side + 1) * channels]
            sigma = 0.5 * jnp.tanh(0.5 * z) + 0.5
            act = z * sigma
            if number + 1 < LAYERS:
                if -SLOPE_PAD[number] <= here < width + SLOPE_PAD[number]:
                    slopes[number][SLOPE_PAD[number] + here] = sigma + act - act * sigma
                following, slot = levels[number + 1], LEVEL_PAD[number + 1] + here
                following[1, slot] = act.astype(BF16)
                fill(following, 2 * dilation, slot, act)
            else:
                slabs[here] = act.astype(BF16)
                signal = columns_up[here].astype(F32) * (sigma + act - act * sigma)
                slot = SIGNAL_PAD[number] + here
                signals[number][1, slot] = signal.astype(BF16)
                fill(signals[number], dilation, slot, signal)

    def backward_columns(number, column, sides):
        dilation = 2**number
        if number + 1 < LAYERS:
            back = backward_part(number, column, range(2 + sides), sides)
        else:
            back = partial[column] + backward_part(number, column, outer)
        for side in range(sides):
            here = column + side * dilation
            value = back[:, side * channels : (side + 1) * channels]
            if number > 0:
                value = value * slopes[number - 1][SLOPE_PAD[number - 1] + here]
                slot = SIGNAL_PAD[number - 1] + here
                signals[number - 1][1, slot] = value.astype(BF16)
                fill(signals[number - 1], dilation // 2, slot, value)
            else:
                slabs[here] = value.astype(BF16)

    def weight_grad(number):
        dilation = 2**number
        pad, level_pad = SIGNAL_PAD[number], LEVEL_PAD[number]
        signal = signals[number][1, pad : pad + width].reshape(rows * width, channels)
        for j in range(3):
            first = level_pad + (j - 1) * dilation
            taken = jnp.concatenate(
                [
                    levels[number][i, first : first + width].reshape(rows * width, channels)
                    for i in range(3)
                ],
                axis=-1,
            )
            total = lax.dot_general(
                signal, taken, (((0,), (0,)), ((), ())), preferred_element_type=F32
            ).astype(BF16)
            for i in range(3):
                send_b[number, :, pl.ds((3 * i + j) * block, block), :] = total[
                    :, i * channels : (i + 1) * channels
                ].reshape(ranks, block, channels)

    def start_batch(number):
        half = ranks // 4
        for step in (half, 3 * half, *(n for n in range(1, ranks) if n not in (half, 3 * half))):
            target = lax.rem(batch + step, ranks)
            pltpu.make_async_remote_copy(
                src_ref=send_b.at[number, target],
                dst_ref=recv_b.at[number, step],
                send_sem=batch_send.at[number],
                recv_sem=batch_recv.at[number],
                device_id={"batch": target},
                device_id_type=MESH,
            ).start()

    sets = ((3, 2), (0, 1))

    lane = lax.broadcasted_iota(jnp.int32, (block, channels), 1)

    def start_lon(which):
        totals = []
        for number in sets[which]:
            arrived = recv_b.at[number, 1:]
            pltpu.make_async_copy(arrived, arrived, batch_recv.at[number]).wait()
            total = send_b[number, batch].astype(F32)
            for step in range(1, ranks):
                total = total + recv_b[number, step].astype(F32)
            totals.append(total)

        def shifted(total, tap, amount):
            value = total[tap * block : (tap + 1) * block]
            return pltpu.roll(value, amount, 1) if amount else value

        for target in range(groups):
            tap, offset = divmod(target * share, channels)
            packed = None
            for place, total in enumerate(totals):
                amount = (place * share - offset) % channels
                value = shifted(total, tap, amount)
                if offset + share > channels:
                    more = shifted(total, tap + 1, amount)
                    value = jnp.where(lane < place * share + channels - offset, value, more)
                packed = value if packed is None else jnp.where(lane < place * share, packed, value)
            send_l[which, target] = packed.astype(BF16)

        @pl.loop(0, groups - 1)
        def _(turn):
            rank = turn // 2
            apart = ((rank + 1) // 2) * (2 * (rank % 2) - 1)
            step = (groups // 4 + (turn % 2) * (groups // 2) + apart + groups) % groups
            target = lax.rem(lon + step, groups)
            pltpu.make_async_remote_copy(
                src_ref=send_l.at[which, target],
                dst_ref=recv_l.at[which, step],
                send_sem=lon_send.at[which],
                recv_sem=lon_recv.at[which],
                device_id={"lon": target},
                device_id_type=MESH,
            ).start()

    def finish(which):
        arrived = recv_l.at[which, 1:]
        pltpu.make_async_copy(arrived, arrived, lon_recv.at[which]).wait()
        total = send_l[which, lon].astype(F32)
        for step in range(1, groups):
            total = total + recv_l[which, step].astype(F32)
        total = total * (1.0 / math.sqrt(rows * width * groups * ranks))
        for place, number in enumerate(sets[which]):
            owned_ref[number] = total[:, place * share : (place + 1) * share]

    fetch_images.wait()
    level, pad = levels[0], LEVEL_PAD[0]
    level[1, pad : pad + width] = swapped(staged[...])
    pl.semaphore_wait(barrier, groups + ranks - 2)
    for piece in range(2):
        for side in range(2):
            halo_copy(0, side, piece).start()
    edge_rows = jnp.zeros((PAD, channels), F32)
    for slot in range(shifter.shape[0]):
        shifter[slot, pl.ds(0, PAD), :] = edge_rows
        shifter[slot, pl.ds(PAD + rows, PAD), :] = edge_rows
    for column in range(width):
        fill(level, 1, pad + column, level[1, pad + column].astype(F32))
    fetch_taps.wait()
    build_forward(0)
    for column in range(2, width - 2, 2):
        forward_pair(0, column)
    build_forward(1)
    for column in (4, 5, 8, 9):
        forward_pair(1, column)
    fetch_upstream.wait()
    columns_up[...] = swapped(upstream[...])
    for number in (2, 3):
        build_forward(number)
    for number in range(LAYERS):
        build_backward(number)
    for half in range(2):
        receive(0, 0, half, 1)
        receive(0, 1, half, 1)
        for place in (2 * half, 2 * half + 1):
            forward_pair(0, -2 * place)
            forward_pair(0, width - 2 + 2 * place)
        for column in ((0, 1, 12, 13), (-4, -3, 16, 17))[half]:
            forward_pair(1, column)
    halves = ((0, 1, 4, 5), (2, 3, 6, 7))
    for half in range(2):
        for column in (0, 8, 1, 9) if half == 0 else (2, 10, 3, 11):
            forward_pair(2, column)
        for piece in (2 * half, 2 * half + 1):
            for side in range(2):
                halo_copy(1, side, piece).start()
    for column in range(8):
        partial[column] = forward_part(3, column, inner)
    for half in range(2):
        for piece in (2 * half, 2 * half + 1):
            receive(1, 0, piece, 8)
            receive(1, 1, piece, 8)
        for column in halves[half]:
            forward_pair(3, column)
        for piece in (2 * half, 2 * half + 1):
            for side in range(2):
                halo_copy(2, side, piece).start()

    for column in range(8):
        partial[column] = backward_part(3, column, inner)
    features_ref[...] = swapped(slabs[...])
    ready = (((0, 0), (0, 1), (1, 0)), ((0, 2), (1, 1), (1, 2)))
    for half in range(2):
        for piece in (2 * half, 2 * half + 1):
            receive(2, 0, piece, 8)
            receive(2, 1, piece, 8)
        for column in halves[half]:
            backward_columns(3, column, 2)
        for side, part in ready[half]:
            halo_copy(3, side, part).start()
    weight_grad(3)
    start_batch(3)
    weight_grad(2)
    start_batch(2)
    for side in range(2):
        for piece in range(3):
            receive(3, side, piece, 4)
    for column in (0, 1, 2, 3, 8, 9, 10, 11):
        backward_columns(2, column, 2)
    for column in (-2, -1, 16, 17):
        backward_columns(2, column, 1)
    for column in (0, 13, 1, 4, 5, 8, 9, 12):
        backward_columns(1, column, 2)
        if column == 13:
            halo_copy(4, 0, 0).start()
            halo_copy(4, 1, 0).start()
    weight_grad(0)
    start_batch(0)
    weight_grad(1)
    start_batch(1)
    start_lon(0)
    receive(4, 0, 0, 1)
    receive(4, 1, 0, 1)
    for column in range(0, width, 2):
        backward_columns(0, column, 2)
    input_grad_ref[...] = swapped(slabs[...])
    start_lon(1)
    for which in range(len(PIECES)):
        for side in range(2):
            for piece in range(len(PIECES[which][side])):
                halo_copy(which, side, piece).wait_send()
    for number in range(LAYERS):
        sent = send_b.at[number, 1:]
        pltpu.make_async_copy(sent, sent, batch_send.at[number]).wait()
    finish(0)
    finish(1)
    for which in range(2):
        sent = send_l.at[which, 1:]
        pltpu.make_async_copy(sent, sent, lon_send.at[which]).wait()


def store(*refs):
    copies = [
        pltpu.make_async_copy(refs[n], refs[3 + n], refs[6].at[n]) for n in range(3)
    ]
    for copy in copies:
        copy.start()
    for copy in copies:
        copy.wait()


def local(images, weights, cotangent):
    _, rows, width, channels = images.shape
    groups, ranks = lax.axis_size("lon"), lax.axis_size("batch")
    block = channels // ranks
    share = 9 * channels // groups
    field = (rows, width, channels)

    def columns(pad, *front):
        return (*front, width + 2 * pad, rows, channels)

    features, input_grad, owned = pl.pallas_call(
        functools.partial(kernel, (groups, ranks)),
        out_shape=(
            pltpu.VMEM(field, BF16),
            pltpu.VMEM(field, BF16),
            pltpu.VMEM((LAYERS, block, share), F32),
        ),
        in_specs=[pl.BlockSpec(memory_space=pl.ANY)] * 3,
        out_specs=(pl.BlockSpec(memory_space=pltpu.VMEM),) * 3,
        scratch_shapes=[
            pltpu.VMEM(field, BF16),
            pltpu.VMEM(field, BF16),
            pltpu.VMEM(columns(0), BF16),
            pltpu.VMEM((LAYERS, 9, channels, channels), BF16),
            pltpu.VMEM((LAYERS, 12 * channels, 2 * channels), BF16),
            pltpu.VMEM((LAYERS, 2 * channels, 12 * channels), BF16),
            pltpu.VMEM((width + 2 * max(LEVEL_PAD), rows + 2 * PAD, channels), F32),
            pltpu.VMEM(columns(0), BF16),
            *[pltpu.VMEM(columns(pad, 3), BF16) for pad in LEVEL_PAD],
            *[pltpu.VMEM(columns(pad, 3), BF16) for pad in SIGNAL_PAD],
            *[pltpu.VMEM(columns(pad), F32) for pad in SLOPE_PAD],
            pltpu.VMEM((LAYERS, ranks, 9 * block, channels), BF16),
            pltpu.VMEM((LAYERS, ranks, 9 * block, channels), BF16),
            pltpu.VMEM((2, groups, block, channels), BF16),
            pltpu.VMEM((2, groups, block, channels), BF16),
            pltpu.VMEM((width // 2, rows, 2 * channels), F32),
            pltpu.SemaphoreType.DMA((3,)),
            pltpu.SemaphoreType.DMA((len(PIECES), 2, 4)),
            pltpu.SemaphoreType.DMA((len(PIECES), 2, 4)),
            pltpu.SemaphoreType.DMA((LAYERS,)),
            pltpu.SemaphoreType.DMA((LAYERS,)),
            pltpu.SemaphoreType.DMA((2,)),
            pltpu.SemaphoreType.DMA((2,)),
        ],
        compiler_params=pltpu.CompilerParams(
            collective_id=0, has_side_effects=True, vmem_limit_bytes=58 * 2**20
        ),
        name="panorama",
    )(images.reshape(field), weights, cotangent.reshape(field))
    features, input_grad, owned = pl.pallas_call(
        store,
        out_shape=(
            jax.ShapeDtypeStruct(field, BF16),
            jax.ShapeDtypeStruct(field, BF16),
            jax.ShapeDtypeStruct((LAYERS, block, share), F32),
        ),
        in_specs=[pl.BlockSpec(memory_space=pltpu.VMEM)] * 3,
        out_specs=[pl.BlockSpec(memory_space=pl.ANY)] * 3,
        scratch_shapes=[pltpu.SemaphoreType.DMA((3,))],
        name="store",
    )(*[pltpu.with_memory_space_constraint(x, pltpu.VMEM) for x in (features, input_grad, owned)])
    weight_grads = jnp.swapaxes(owned, 1, 2)
    return features.reshape(images.shape), input_grad.reshape(images.shape), weight_grads


def solution(mesh):
    return jax.shard_map(
        local,
        mesh=mesh,
        in_specs=(P("batch", None, "lon", None), P(), P("batch", None, "lon", None)),
        out_specs=(
            P("batch", None, "lon", None),
            P("batch", None, "lon", None),
            P(None, "lon", "batch"),
        ),
        check_vma=False,
    )
```

```python
import functools
import math

import jax
import jax.numpy as jnp
from jax import lax
from jax.experimental import pallas as pl
from jax.experimental.pallas import tpu as pltpu
from jax.sharding import PartitionSpec as P

LAYERS = 4
PAD = 8
BF16 = jnp.bfloat16
F32 = jnp.float32
MESH = pl.DeviceIdType.MESH

LEVEL_PAD = (7, 6, 4, 8)
SIGNAL_PAD = (1, 2, 6, 8)
SLOPE_PAD = (0, 2, 0)
PIECES = (
    (((0, 3), (3, 4)), ((13, 3), (9, 4))),
    (((0, 2), (4, 2), (2, 2), (6, 2)), ((8, 2), (12, 2), (10, 2), (14, 2))),
    (((0, 2), (4, 2), (2, 2), (6, 2)), ((8, 2), (12, 2), (10, 2), (14, 2))),
    (((0, 2), (4, 2), (2, 2)), ((12, 2), (10, 2), (14, 2))),
    (((0, 1),), ((15, 1),)),
)


def swapped(value):
    return jnp.swapaxes(value, 0, 1)


def kernel(
    ring, images_ref, weights_ref, cotangent_ref, features_ref, input_grad_ref, owned_ref, *scratch
):
    groups, ranks = ring
    (staged, upstream, columns_up, taps, forward_w, backward_w, shifter, slabs) = scratch[:8]
    levels = scratch[8:12]
    signals = scratch[12:16]
    slopes = scratch[16:19]
    send_b, recv_b, send_l, recv_l, partial, local_sem = scratch[19:25]
    halo_send, halo_recv, batch_send, batch_recv, lon_send, lon_recv, known = scratch[25:32]

    lon = lax.axis_index("lon")
    batch = lax.axis_index("batch")
    right, left = lax.rem(lon + 1, groups), lax.rem(lon + groups - 1, groups)
    rows, width, channels = staged.shape
    block = channels // ranks
    share = 9 * channels // groups

    barrier = pltpu.get_barrier_semaphore()
    axes = (("lon", lon, groups), ("batch", batch, ranks))

    def tell(semaphore, which, apart):
        name, here, size = axes[which]
        for peer in (lax.rem(here + apart, size), lax.rem(here + size - apart, size)):
            pl.semaphore_signal(semaphore, inc=1, device_id={name: peer}, device_id_type=MESH)

    def tell_round(turn):
        for which, (_, _, size) in enumerate(axes):
            if 4 * 2**turn <= size:
                tell(known.at[which, turn], which, 2**turn)

    def hear_round(turn):
        for which, (_, _, size) in enumerate(axes):
            if 4 * 2**turn <= size:
                pl.semaphore_wait(known.at[which, turn], 2)

    fetch_images = pltpu.make_async_copy(images_ref, staged, local_sem.at[0])
    fetch_taps = pltpu.make_async_copy(weights_ref, taps, local_sem.at[1])
    fetch_upstream = pltpu.make_async_copy(cotangent_ref, upstream, local_sem.at[2])
    fetch_images.start()
    tell(barrier, 0, 1)
    tell(barrier, 1, 1)
    fetch_taps.start()
    fetch_upstream.start()

    exchanged = (
        (levels[0], LEVEL_PAD[0]),
        (levels[3], LEVEL_PAD[3]),
        (signals[3], SIGNAL_PAD[3]),
        (signals[2], SIGNAL_PAD[2]),
        (signals[0], SIGNAL_PAD[0]),
    )

    def halo_copy(which, side, piece):
        buffer, pad = exchanged[which]
        first, count = PIECES[which][side][piece]
        landing = first + width if side == 0 else first - width
        return pltpu.make_async_remote_copy(
            src_ref=buffer.at[1, pad + first : pad + first + count],
            dst_ref=buffer.at[1, pad + landing : pad + landing + count],
            send_sem=halo_send.at[which, side, piece],
            recv_sem=halo_recv.at[which, side, piece],
            device_id={"lon": left if side == 0 else right},
            device_id_type=MESH,
        )

    def fill(buffer, dilation, slot, value):
        shifter[slot, pl.ds(PAD, rows), :] = value
        buffer[0, slot] = shifter[slot, pl.ds(PAD - dilation, rows), :].astype(BF16)
        buffer[2, slot] = shifter[slot, pl.ds(PAD + dilation, rows), :].astype(BF16)

    def receive(which, side, piece, dilation):
        buffer, pad = exchanged[which]
        halo_copy(which, side, piece).wait_recv()
        first, count = PIECES[which][side][piece]
        landing = pad + (first + width if side == 0 else first - width)
        for slot in range(landing, landing + count):
            fill(buffer, dilation, slot, buffer[1, slot].astype(F32))

    def tap_block(number, tap_row, tap_column, turned):
        if not 0 <= tap_column < 3:
            return jnp.zeros((channels, channels), BF16)
        tap = 3 * tap_row + tap_column
        return taps[number, 8 - tap if turned else tap]

    def build_forward(number):
        for span in range(4):
            for row in range(3):
                for side in range(2):
                    forward_w[
                        number,
                        pl.ds((3 * span + row) * channels, channels),
                        pl.ds(side * channels, channels),
                    ] = tap_block(number, row, span - side, False)

    def build_backward(number):
        for span in range(4):
            for row in range(3):
                for side in range(2):
                    backward_w[
                        number,
                        pl.ds(side * channels, channels),
                        pl.ds((3 * span + row) * channels, channels),
                    ] = tap_block(number, row, span - side, True)

    def gathered(buffer, pad, dilation, column, spans=range(4)):
        return jnp.concatenate(
            [
                buffer[row, pad + column + (span - 1) * dilation]
                for span in spans
                for row in range(3)
            ],
            axis=-1,
        )

    inner, outer = (1, 2), (0, 3)
    third = 3 * channels

    def forward_part(number, column, spans):
        return jnp.dot(
            gathered(levels[number], LEVEL_PAD[number], 2**number, column, spans),
            jnp.concatenate([forward_w[number, pl.ds(span * third, third), :] for span in spans], axis=0),
            preferred_element_type=F32,
        )

    def backward_part(number, column, spans, sides=2):
        return lax.dot_general(
            gathered(signals[number], SIGNAL_PAD[number], 2**number, column, spans),
            jnp.concatenate(
                [
                    backward_w[number, pl.ds(0, sides * channels), pl.ds(span * third, third)]
                    for span in spans
                ],
                axis=1,
            ),
            (((1,), (1,)), ((), ())),
            preferred_element_type=F32,
        )

    def forward_pair(number, column):
        dilation = 2**number
        if number + 1 < LAYERS:
            summed = forward_part(number, column, range(4))
        else:
            summed = partial[column] + forward_part(number, column, outer)
        for side in range(2):
            here = column + side * dilation
            z = summed[:, side * channels : (side + 1) * channels]
            sigma = 0.5 * jnp.tanh(0.5 * z) + 0.5
            act = z * sigma
            if number + 1 < LAYERS:
                if -SLOPE_PAD[number] <= here < width + SLOPE_PAD[number]:
                    slopes[number][SLOPE_PAD[number] + here] = sigma + act - act * sigma
                following, slot = levels[number + 1], LEVEL_PAD[number + 1] + here
                following[1, slot] = act.astype(BF16)
                fill(following, 2 * dilation, slot, act)
            else:
                slabs[here] = act.astype(BF16)
                signal = columns_up[here].astype(F32) * (sigma + act - act * sigma)
                slot = SIGNAL_PAD[number] + here
                signals[number][1, slot] = signal.astype(BF16)
                fill(signals[number], dilation, slot, signal)

    def backward_columns(number, column, sides):
        dilation = 2**number
        if number + 1 < LAYERS:
            back = backward_part(number, column, range(2 + sides), sides)
        else:
            back = partial[column] + backward_part(number, column, outer)
        for side in range(sides):
            here = column + side * dilation
            value = back[:, side * channels : (side + 1) * channels]
            if number > 0:
                value = value * slopes[number - 1][SLOPE_PAD[number - 1] + here]
                slot = SIGNAL_PAD[number - 1] + here
                signals[number - 1][1, slot] = value.astype(BF16)
                fill(signals[number - 1], dilation // 2, slot, value)
            else:
                slabs[here] = value.astype(BF16)

    def weight_grad(number, cut=None):
        dilation = 2**number
        pad, level_pad = SIGNAL_PAD[number], LEVEL_PAD[number]
        signal = signals[number][1, pad : pad + width].reshape(rows * width, channels)
        for j in range(3):
            first = level_pad + (j - 1) * dilation
            taken = jnp.concatenate(
                [
                    levels[number][i, first : first + width].reshape(rows * width, channels)
                    for i in range(3)
                ],
                axis=-1,
            )
            total = lax.dot_general(
                signal, taken, (((0,), (0,)), ((), ())), preferred_element_type=F32
            ).astype(BF16)
            for i in range(3):
                send_b[number, :, pl.ds((3 * j + i) * block, block), :] = total[
                    :, i * channels : (i + 1) * channels
                ].reshape(ranks, block, channels)
            if cut is not None and j + 1 == cut:
                start_batch(number, 0, cut)
        start_batch(number, cut or 0, 3)

    def start_batch(number, first, last):
        half = ranks // 4
        for step in (half, 3 * half, *(n for n in range(1, ranks) if n not in (half, 3 * half))):
            target = lax.rem(batch + step, ranks)
            pltpu.make_async_remote_copy(
                src_ref=send_b.at[number, target, pl.ds(3 * first * block, 3 * (last - first) * block)],
                dst_ref=recv_b.at[number, step, pl.ds(3 * first * block, 3 * (last - first) * block)],
                send_sem=batch_send.at[number],
                recv_sem=batch_recv.at[number],
                device_id={"batch": target},
                device_id_type=MESH,
            ).start()

    sets = ((3, 2), (0, 1))

    lane = lax.broadcasted_iota(jnp.int32, (block, channels), 1)

    def start_lon(which):
        totals = []
        for number in sets[which]:
            arrived = recv_b.at[number, 1:]
            pltpu.make_async_copy(arrived, arrived, batch_recv.at[number]).wait()
            total = send_b[number, batch].astype(F32)
            for step in range(1, ranks):
                total = total + recv_b[number, step].astype(F32)
            totals.append(total)

        def shifted(total, tap, amount):
            place = 3 * (tap % 3) + tap // 3
            value = total[place * block : (place + 1) * block]
            return pltpu.roll(value, amount, 1) if amount else value

        for target in range(groups):
            tap, offset = divmod(target * share, channels)
            packed = None
            for place, total in enumerate(totals):
                amount = (place * share - offset) % channels
                value = shifted(total, tap, amount)
                if offset + share > channels:
                    more = shifted(total, tap + 1, amount)
                    value = jnp.where(lane < place * share + channels - offset, value, more)
                packed = value if packed is None else jnp.where(lane < place * share, packed, value)
            send_l[which, target] = packed.astype(BF16)

        @pl.loop(0, groups - 1)
        def _(turn):
            rank = turn // 2
            apart = ((rank + 1) // 2) * (2 * (rank % 2) - 1)
            step = (groups // 4 + (turn % 2) * (groups // 2) + apart + groups) % groups
            target = lax.rem(lon + step, groups)
            pltpu.make_async_remote_copy(
                src_ref=send_l.at[which, target],
                dst_ref=recv_l.at[which, step],
                send_sem=lon_send.at[which],
                recv_sem=lon_recv.at[which],
                device_id={"lon": target},
                device_id_type=MESH,
            ).start()

    def finish(which):
        arrived = recv_l.at[which, 1:]
        pltpu.make_async_copy(arrived, arrived, lon_recv.at[which]).wait()
        total = send_l[which, lon].astype(F32)
        for step in range(1, groups):
            total = total + recv_l[which, step].astype(F32)
        total = total * (1.0 / math.sqrt(rows * width * groups * ranks))
        for place, number in enumerate(sets[which]):
            owned_ref[number] = total[:, place * share : (place + 1) * share]

    fetch_images.wait()
    level, pad = levels[0], LEVEL_PAD[0]
    level[1, pad : pad + width] = swapped(staged[...])
    pl.semaphore_wait(barrier, 4)
    for piece in range(2):
        for side in range(2):
            halo_copy(0, side, piece).start()
    tell_round(0)
    edge_rows = jnp.zeros((PAD, channels), F32)
    for slot in range(shifter.shape[0]):
        shifter[slot, pl.ds(0, PAD), :] = edge_rows
        shifter[slot, pl.ds(PAD + rows, PAD), :] = edge_rows
    for column in range(width):
        fill(level, 1, pad + column, level[1, pad + column].astype(F32))
    fetch_taps.wait()
    build_forward(0)
    for column in range(2, width - 2, 2):
        forward_pair(0, column)
    build_forward(1)
    for column in (4, 5, 8, 9):
        forward_pair(1, column)
    fetch_upstream.wait()
    columns_up[...] = swapped(upstream[...])
    for number in (2, 3):
        build_forward(number)
    for number in range(LAYERS):
        build_backward(number)
    hear_round(0)
    tell_round(1)
    for half in range(2):
        receive(0, 0, half, 1)
        receive(0, 1, half, 1)
        for place in (2 * half, 2 * half + 1):
            forward_pair(0, -2 * place)
            forward_pair(0, width - 2 + 2 * place)
        for column in ((0, 1, 12, 13), (-4, -3, 16, 17))[half]:
            forward_pair(1, column)
    halves = ((0, 1, 4, 5), (2, 3, 6, 7))
    for half in range(2):
        for column in (0, 8, 1, 9) if half == 0 else (2, 10, 3, 11):
            forward_pair(2, column)
        for piece in (2 * half, 2 * half + 1):
            for side in range(2):
                halo_copy(1, side, piece).start()
    for column in range(8):
        partial[column] = forward_part(3, column, inner)
    hear_round(1)
    tell_round(2)
    for half in range(2):
        for piece in (2 * half, 2 * half + 1):
            receive(1, 0, piece, 8)
            receive(1, 1, piece, 8)
        for column in halves[half]:
            forward_pair(3, column)
        for piece in (2 * half, 2 * half + 1):
            for side in range(2):
                halo_copy(2, side, piece).start()

    for column in range(8):
        partial[column] = backward_part(3, column, inner)
    features_ref[...] = swapped(slabs[...])
    ready = (((0, 0), (0, 1), (1, 0)), ((0, 2), (1, 1), (1, 2)))
    hear_round(2)
    tell_round(3)
    for half in range(2):
        for piece in (2 * half, 2 * half + 1):
            receive(2, 0, piece, 8)
            receive(2, 1, piece, 8)
        for column in halves[half]:
            backward_columns(3, column, 2)
        for side, part in ready[half]:
            halo_copy(3, side, part).start()
    weight_grad(3)
    weight_grad(2)
    for side in range(2):
        for piece in range(3):
            receive(3, side, piece, 4)
    for column in (0, 1, 2, 3, 8, 9, 10, 11):
        backward_columns(2, column, 2)
    for column in (-2, -1, 16, 17):
        backward_columns(2, column, 1)
    for column in (0, 13, 1, 4, 5, 8, 9, 12):
        backward_columns(1, column, 2)
        if column == 13:
            halo_copy(4, 0, 0).start()
            halo_copy(4, 1, 0).start()
    weight_grad(0)
    weight_grad(1, 2)
    hear_round(3)
    start_lon(0)
    start_lon(1)
    receive(4, 0, 0, 1)
    receive(4, 1, 0, 1)
    for column in range(0, width, 2):
        backward_columns(0, column, 2)
    input_grad_ref[...] = swapped(slabs[...])

    for which in range(len(PIECES)):
        for side in range(2):
            for piece in range(len(PIECES[which][side])):
                halo_copy(which, side, piece).wait_send()
    for number in range(LAYERS):
        sent = send_b.at[number, 1:]
        pltpu.make_async_copy(sent, sent, batch_send.at[number]).wait()
    finish(0)
    finish(1)
    for which in range(2):
        sent = send_l.at[which, 1:]
        pltpu.make_async_copy(sent, sent, lon_send.at[which]).wait()


def store(*refs):
    copies = [
        pltpu.make_async_copy(refs[n], refs[3 + n], refs[6].at[n]) for n in range(3)
    ]
    for copy in copies:
        copy.start()
    for copy in copies:
        copy.wait()


def local(images, weights, cotangent):
    _, rows, width, channels = images.shape
    groups, ranks = lax.axis_size("lon"), lax.axis_size("batch")
    block = channels // ranks
    share = 9 * channels // groups
    field = (rows, width, channels)

    def columns(pad, *front):
        return (*front, width + 2 * pad, rows, channels)

    features, input_grad, owned = pl.pallas_call(
        functools.partial(kernel, (groups, ranks)),
        out_shape=(
            pltpu.VMEM(field, BF16),
            pltpu.VMEM(field, BF16),
            pltpu.VMEM((LAYERS, block, share), F32),
        ),
        in_specs=[pl.BlockSpec(memory_space=pl.ANY)] * 3,
        out_specs=(pl.BlockSpec(memory_space=pltpu.VMEM),) * 3,
        scratch_shapes=[
            pltpu.VMEM(field, BF16),
            pltpu.VMEM(field, BF16),
            pltpu.VMEM(columns(0), BF16),
            pltpu.VMEM((LAYERS, 9, channels, channels), BF16),
            pltpu.VMEM((LAYERS, 12 * channels, 2 * channels), BF16),
            pltpu.VMEM((LAYERS, 2 * channels, 12 * channels), BF16),
            pltpu.VMEM((width + 2 * max(LEVEL_PAD), rows + 2 * PAD, channels), F32),
            pltpu.VMEM(columns(0), BF16),
            *[pltpu.VMEM(columns(pad, 3), BF16) for pad in LEVEL_PAD],
            *[pltpu.VMEM(columns(pad, 3), BF16) for pad in SIGNAL_PAD],
            *[pltpu.VMEM(columns(pad), F32) for pad in SLOPE_PAD],
            pltpu.VMEM((LAYERS, ranks, 9 * block, channels), BF16),
            pltpu.VMEM((LAYERS, ranks, 9 * block, channels), BF16),
            pltpu.VMEM((2, groups, block, channels), BF16),
            pltpu.VMEM((2, groups, block, channels), BF16),
            pltpu.VMEM((width // 2, rows, 2 * channels), F32),
            pltpu.SemaphoreType.DMA((3,)),
            pltpu.SemaphoreType.DMA((len(PIECES), 2, 4)),
            pltpu.SemaphoreType.DMA((len(PIECES), 2, 4)),
            pltpu.SemaphoreType.DMA((LAYERS,)),
            pltpu.SemaphoreType.DMA((LAYERS,)),
            pltpu.SemaphoreType.DMA((2,)),
            pltpu.SemaphoreType.DMA((2,)),
            pltpu.SemaphoreType.REGULAR((2, 4)),
        ],
        compiler_params=pltpu.CompilerParams(
            collective_id=0, has_side_effects=True, vmem_limit_bytes=58 * 2**20
        ),
        name="panorama",
    )(images.reshape(field), weights, cotangent.reshape(field))
    features, input_grad, owned = pl.pallas_call(
        store,
        out_shape=(
            jax.ShapeDtypeStruct(field, BF16),
            jax.ShapeDtypeStruct(field, BF16),
            jax.ShapeDtypeStruct((LAYERS, block, share), F32),
        ),
        in_specs=[pl.BlockSpec(memory_space=pltpu.VMEM)] * 3,
        out_specs=[pl.BlockSpec(memory_space=pl.ANY)] * 3,
        scratch_shapes=[pltpu.SemaphoreType.DMA((3,))],
        name="store",
    )(*[pltpu.with_memory_space_constraint(x, pltpu.VMEM) for x in (features, input_grad, owned)])
    weight_grads = jnp.swapaxes(owned, 1, 2)
    return features.reshape(images.shape), input_grad.reshape(images.shape), weight_grads


def solution(mesh):
    return jax.shard_map(
        local,
        mesh=mesh,
        in_specs=(P("batch", None, "lon", None), P(), P("batch", None, "lon", None)),
        out_specs=(
            P("batch", None, "lon", None),
            P("batch", None, "lon", None),
            P(None, "lon", "batch"),
        ),
        check_vma=False,
    )
```

```python
import functools
import math

import jax
import jax.numpy as jnp
from jax import lax
from jax.experimental import pallas as pl
from jax.experimental.pallas import tpu as pltpu
from jax.sharding import PartitionSpec as P

LAYERS = 4
PAD = 8
BF16 = jnp.bfloat16
F32 = jnp.float32
MESH = pl.DeviceIdType.MESH

LEVEL_PAD = (7, 6, 4, 8)
SIGNAL_PAD = (1, 2, 6, 8)
SLOPE_PAD = (0, 2, 0)
PIECES = (
    (((0, 3), (3, 4)), ((13, 3), (9, 4))),
    (((0, 2), (4, 2), (2, 2), (6, 2)), ((8, 2), (12, 2), (10, 2), (14, 2))),
    (((0, 2), (4, 2), (2, 2), (6, 2)), ((8, 2), (12, 2), (10, 2), (14, 2))),
    (((0, 2), (4, 2), (2, 2)), ((12, 2), (10, 2), (14, 2))),
    (((0, 1),), ((15, 1),)),
)


def swapped(value):
    return jnp.swapaxes(value, 0, 1)


def kernel(
    ring, images_ref, weights_ref, cotangent_ref, features_ref, input_grad_ref, owned_ref, *scratch
):
    groups, ranks = ring
    (staged, upstream, columns_up, taps, forward_w, backward_w, shifter, slabs) = scratch[:8]
    levels = scratch[8:12]
    signals = scratch[12:16]
    slopes = scratch[16:19]
    send_b, recv_b, send_l, recv_l, partial, local_sem = scratch[19:25]
    halo_send, halo_recv, batch_send, batch_recv, lon_send, lon_recv, known = scratch[25:32]

    lon = lax.axis_index("lon")
    batch = lax.axis_index("batch")
    right, left = lax.rem(lon + 1, groups), lax.rem(lon + groups - 1, groups)
    rows, width, channels = staged.shape
    block = channels // ranks
    share = 9 * channels // groups

    barrier = pltpu.get_barrier_semaphore()
    axes = (("lon", lon, groups), ("batch", batch, ranks))

    def tell(semaphore, which, apart):
        name, here, size = axes[which]
        for peer in (lax.rem(here + apart, size), lax.rem(here + size - apart, size)):
            pl.semaphore_signal(semaphore, inc=1, device_id={name: peer}, device_id_type=MESH)

    def tell_round(turn):
        for which, (_, _, size) in enumerate(axes):
            if 4 * 2**turn <= size:
                tell(known.at[which, turn], which, 2**turn)

    def hear_round(turn):
        for which, (_, _, size) in enumerate(axes):
            if 4 * 2**turn <= size:
                pl.semaphore_wait(known.at[which, turn], 2)

    fetch_images = pltpu.make_async_copy(images_ref, staged, local_sem.at[0])
    fetch_taps = pltpu.make_async_copy(weights_ref, taps, local_sem.at[1])
    fetch_upstream = pltpu.make_async_copy(cotangent_ref, upstream, local_sem.at[2])
    fetch_images.start()
    tell(barrier, 0, 1)
    tell(barrier, 1, 1)
    fetch_taps.start()
    fetch_upstream.start()

    exchanged = (
        (levels[0], LEVEL_PAD[0]),
        (levels[3], LEVEL_PAD[3]),
        (signals[3], SIGNAL_PAD[3]),
        (signals[2], SIGNAL_PAD[2]),
        (signals[0], SIGNAL_PAD[0]),
    )

    def halo_copy(which, side, piece):
        buffer, pad = exchanged[which]
        first, count = PIECES[which][side][piece]
        landing = first + width if side == 0 else first - width
        return pltpu.make_async_remote_copy(
            src_ref=buffer.at[1, pad + first : pad + first + count],
            dst_ref=buffer.at[1, pad + landing : pad + landing + count],
            send_sem=halo_send.at[which, side, piece],
            recv_sem=halo_recv.at[which, side, piece],
            device_id={"lon": left if side == 0 else right},
            device_id_type=MESH,
        )

    def fill(buffer, dilation, slot, value):
        shifter[slot, pl.ds(PAD, rows), :] = value
        buffer[0, slot] = shifter[slot, pl.ds(PAD - dilation, rows), :].astype(BF16)
        buffer[2, slot] = shifter[slot, pl.ds(PAD + dilation, rows), :].astype(BF16)

    def receive(which, side, piece, dilation):
        buffer, pad = exchanged[which]
        halo_copy(which, side, piece).wait_recv()
        first, count = PIECES[which][side][piece]
        landing = pad + (first + width if side == 0 else first - width)
        for slot in range(landing, landing + count):
            fill(buffer, dilation, slot, buffer[1, slot].astype(F32))

    def tap_block(number, tap_row, tap_column, turned):
        if not 0 <= tap_column < 3:
            return jnp.zeros((channels, channels), BF16)
        tap = 3 * tap_row + tap_column
        return taps[number, 8 - tap if turned else tap]

    def build_forward(number):
        for span in range(4):
            for row in range(3):
                for side in range(2):
                    forward_w[
                        number,
                        pl.ds((3 * span + row) * channels, channels),
                        pl.ds(side * channels, channels),
                    ] = tap_block(number, row, span - side, False)

    def build_backward(number):
        for span in range(4):
            for row in range(3):
                for side in range(2):
                    backward_w[
                        number,
                        pl.ds(side * channels, channels),
                        pl.ds((3 * span + row) * channels, channels),
                    ] = tap_block(number, row, span - side, True)

    def gathered(buffer, pad, dilation, column, spans=range(4)):
        return jnp.concatenate(
            [
                buffer[row, pad + column + (span - 1) * dilation]
                for span in spans
                for row in range(3)
            ],
            axis=-1,
        )

    inner, outer = (1, 2), (0, 3)
    third = 3 * channels

    def forward_part(number, column, spans):
        return jnp.dot(
            gathered(levels[number], LEVEL_PAD[number], 2**number, column, spans),
            jnp.concatenate([forward_w[number, pl.ds(span * third, third), :] for span in spans], axis=0),
            preferred_element_type=F32,
        )

    def backward_part(number, column, spans, sides=2):
        return lax.dot_general(
            gathered(signals[number], SIGNAL_PAD[number], 2**number, column, spans),
            jnp.concatenate(
                [
                    backward_w[number, pl.ds(0, sides * channels), pl.ds(span * third, third)]
                    for span in spans
                ],
                axis=1,
            ),
            (((1,), (1,)), ((), ())),
            preferred_element_type=F32,
        )

    def forward_pair(number, column):
        dilation = 2**number
        if number + 1 < LAYERS:
            summed = forward_part(number, column, range(4))
        else:
            summed = partial[column] + forward_part(number, column, outer)
        for side in range(2):
            here = column + side * dilation
            z = summed[:, side * channels : (side + 1) * channels]
            sigma = 0.5 * jnp.tanh(0.5 * z) + 0.5
            act = z * sigma
            if number + 1 < LAYERS:
                if -SLOPE_PAD[number] <= here < width + SLOPE_PAD[number]:
                    slopes[number][SLOPE_PAD[number] + here] = sigma + act - act * sigma
                following, slot = levels[number + 1], LEVEL_PAD[number + 1] + here
                following[1, slot] = act.astype(BF16)
                fill(following, 2 * dilation, slot, act)
            else:
                slabs[here] = act.astype(BF16)
                signal = columns_up[here].astype(F32) * (sigma + act - act * sigma)
                slot = SIGNAL_PAD[number] + here
                signals[number][1, slot] = signal.astype(BF16)
                fill(signals[number], dilation, slot, signal)

    def backward_columns(number, column, sides):
        dilation = 2**number
        if number == 2 and sides == 2:
            outside = (0,) if column < dilation else (3,)
            back = partial[column % 8 + column // 8 * 4] + backward_part(number, column, outside)
        elif number + 1 < LAYERS:
            back = backward_part(number, column, range(2 + sides), sides)
        else:
            back = partial[column] + backward_part(number, column, outer)
        for side in range(sides):
            here = column + side * dilation
            value = back[:, side * channels : (side + 1) * channels]
            if number > 0:
                value = value * slopes[number - 1][SLOPE_PAD[number - 1] + here]
                slot = SIGNAL_PAD[number - 1] + here
                signals[number - 1][1, slot] = value.astype(BF16)
                fill(signals[number - 1], dilation // 2, slot, value)
            else:
                slabs[here] = value.astype(BF16)

    def weight_grad(number, cut=None):
        dilation = 2**number
        pad, level_pad = SIGNAL_PAD[number], LEVEL_PAD[number]
        signal = signals[number][1, pad : pad + width].reshape(rows * width, channels)
        for j in range(3):
            first = level_pad + (j - 1) * dilation
            taken = jnp.concatenate(
                [
                    levels[number][i, first : first + width].reshape(rows * width, channels)
                    for i in range(3)
                ],
                axis=-1,
            )
            total = lax.dot_general(
                signal, taken, (((0,), (0,)), ((), ())), preferred_element_type=F32
            ).astype(BF16)
            for i in range(3):
                send_b[number, :, pl.ds((3 * j + i) * block, block), :] = total[
                    :, i * channels : (i + 1) * channels
                ].reshape(ranks, block, channels)
            if cut is not None and j + 1 == cut:
                start_batch(number, 0, cut)
        start_batch(number, cut or 0, 3)

    def start_batch(number, first, last):
        half = ranks // 4
        for step in (half, 3 * half, *(n for n in range(1, ranks) if n not in (half, 3 * half))):
            target = lax.rem(batch + step, ranks)
            pltpu.make_async_remote_copy(
                src_ref=send_b.at[number, target, pl.ds(3 * first * block, 3 * (last - first) * block)],
                dst_ref=recv_b.at[number, step, pl.ds(3 * first * block, 3 * (last - first) * block)],
                send_sem=batch_send.at[number],
                recv_sem=batch_recv.at[number],
                device_id={"batch": target},
                device_id_type=MESH,
            ).start()

    sets = ((3, 2), (0, 1))

    lane = lax.broadcasted_iota(jnp.int32, (block, channels), 1)

    def start_lon(which):
        totals = []
        for number in sets[which]:
            arrived = recv_b.at[number, 1:]
            pltpu.make_async_copy(arrived, arrived, batch_recv.at[number]).wait()
            total = send_b[number, batch].astype(F32)
            for step in range(1, ranks):
                total = total + recv_b[number, step].astype(F32)
            totals.append(total)

        def shifted(total, tap, amount):
            place = 3 * (tap % 3) + tap // 3
            value = total[place * block : (place + 1) * block]
            return pltpu.roll(value, amount, 1) if amount else value

        for target in range(groups):
            tap, offset = divmod(target * share, channels)
            packed = None
            for place, total in enumerate(totals):
                amount = (place * share - offset) % channels
                value = shifted(total, tap, amount)
                if offset + share > channels:
                    more = shifted(total, tap + 1, amount)
                    value = jnp.where(lane < place * share + channels - offset, value, more)
                packed = value if packed is None else jnp.where(lane < place * share, packed, value)
            send_l[which, target] = packed.astype(BF16)

        @pl.loop(0, groups - 1)
        def _(turn):
            rank = turn // 2
            apart = ((rank + 1) // 2) * (2 * (rank % 2) - 1)
            step = (groups // 4 + (turn % 2) * (groups // 2) + apart + groups) % groups
            target = lax.rem(lon + step, groups)
            pltpu.make_async_remote_copy(
                src_ref=send_l.at[which, target],
                dst_ref=recv_l.at[which, step],
                send_sem=lon_send.at[which],
                recv_sem=lon_recv.at[which],
                device_id={"lon": target},
                device_id_type=MESH,
            ).start()

    def finish(which):
        arrived = recv_l.at[which, 1:]
        pltpu.make_async_copy(arrived, arrived, lon_recv.at[which]).wait()
        total = send_l[which, lon].astype(F32)
        for step in range(1, groups):
            total = total + recv_l[which, step].astype(F32)
        total = total * (1.0 / math.sqrt(rows * width * groups * ranks))
        for place, number in enumerate(sets[which]):
            owned_ref[number] = total[:, place * share : (place + 1) * share]

    fetch_images.wait()
    level, pad = levels[0], LEVEL_PAD[0]
    level[1, pad : pad + width] = swapped(staged[...])
    pl.semaphore_wait(barrier, 4)
    for piece in range(2):
        for side in range(2):
            halo_copy(0, side, piece).start()
    tell_round(0)
    edge_rows = jnp.zeros((PAD, channels), F32)
    for slot in range(shifter.shape[0]):
        shifter[slot, pl.ds(0, PAD), :] = edge_rows
        shifter[slot, pl.ds(PAD + rows, PAD), :] = edge_rows
    for column in range(width):
        fill(level, 1, pad + column, level[1, pad + column].astype(F32))
    fetch_taps.wait()
    build_forward(0)
    for column in range(2, width - 2, 2):
        forward_pair(0, column)
    build_forward(1)
    for column in (4, 5, 8, 9):
        forward_pair(1, column)
    fetch_upstream.wait()
    columns_up[...] = swapped(upstream[...])
    for number in (2, 3):
        build_forward(number)
    for number in range(LAYERS):
        build_backward(number)
    hear_round(0)
    tell_round(1)
    for half in range(2):
        receive(0, 0, half, 1)
        receive(0, 1, half, 1)
        for place in (2 * half, 2 * half + 1):
            forward_pair(0, -2 * place)
            forward_pair(0, width - 2 + 2 * place)
        for column in ((0, 1, 12, 13), (-4, -3, 16, 17))[half]:
            forward_pair(1, column)
    firsts = (0, 4, 2, 6)
    for half in range(2):
        for side in range(2):
            for column in (2 * half, 2 * half + 1):
                forward_pair(2, column + 8 * side)
            for piece in (2 * half, 2 * half + 1):
                halo_copy(1, side, piece).start()
    for column in range(8):
        partial[column] = forward_part(3, column, inner)
    hear_round(1)
    tell_round(2)
    for piece, first in enumerate(firsts):
        for side in range(2):
            receive(1, side, piece, 8)
        for column in (first, first + 1):
            forward_pair(3, column)
        for side in range(2):
            halo_copy(2, side, piece).start()

    for column in range(8):
        partial[column] = backward_part(3, column, inner)
    features_ref[...] = swapped(slabs[...])
    ready = (((0, 0),), ((0, 1), (1, 0)), ((0, 2), (1, 1)), ((1, 2),))
    hear_round(2)
    tell_round(3)
    for piece, first in enumerate(firsts):
        for side in range(2):
            receive(2, side, piece, 8)
        for column in (first, first + 1):
            backward_columns(3, column, 2)
        for side, part in ready[piece]:
            halo_copy(3, side, part).start()
    weight_grad(3)
    weight_grad(2)
    for column in (0, 1, 2, 3, 8, 9, 10, 11):
        partial[column % 8 + column // 8 * 4] = backward_part(
            2, column, (1, 2, 3) if column < 4 else (0, 1, 2)
        )
    for side in range(2):
        for piece in range(3):
            receive(3, side, piece, 4)
    for column in (0, 1, 2, 3, 8, 9, 10, 11):
        backward_columns(2, column, 2)
    for column in (-2, -1, 16, 17):
        backward_columns(2, column, 1)
    for column in (0, 13, 1, 4, 5, 8, 9, 12):
        backward_columns(1, column, 2)
        if column == 13:
            halo_copy(4, 0, 0).start()
            halo_copy(4, 1, 0).start()
    weight_grad(0)
    weight_grad(1, 2)
    hear_round(3)
    start_lon(0)
    start_lon(1)
    receive(4, 0, 0, 1)
    receive(4, 1, 0, 1)
    for column in range(0, width, 2):
        backward_columns(0, column, 2)
    input_grad_ref[...] = swapped(slabs[...])

    for which in range(len(PIECES)):
        for side in range(2):
            for piece in range(len(PIECES[which][side])):
                halo_copy(which, side, piece).wait_send()
    for number in range(LAYERS):
        sent = send_b.at[number, 1:]
        pltpu.make_async_copy(sent, sent, batch_send.at[number]).wait()
    finish(0)
    finish(1)
    for which in range(2):
        sent = send_l.at[which, 1:]
        pltpu.make_async_copy(sent, sent, lon_send.at[which]).wait()


def store(*refs):
    copies = [
        pltpu.make_async_copy(refs[n], refs[3 + n], refs[6].at[n]) for n in range(3)
    ]
    for copy in copies:
        copy.start()
    for copy in copies:
        copy.wait()


def local(images, weights, cotangent):
    _, rows, width, channels = images.shape
    groups, ranks = lax.axis_size("lon"), lax.axis_size("batch")
    block = channels // ranks
    share = 9 * channels // groups
    field = (rows, width, channels)

    def columns(pad, *front):
        return (*front, width + 2 * pad, rows, channels)

    features, input_grad, owned = pl.pallas_call(
        functools.partial(kernel, (groups, ranks)),
        out_shape=(
            pltpu.VMEM(field, BF16),
            pltpu.VMEM(field, BF16),
            pltpu.VMEM((LAYERS, block, share), F32),
        ),
        in_specs=[pl.BlockSpec(memory_space=pl.ANY)] * 3,
        out_specs=(pl.BlockSpec(memory_space=pltpu.VMEM),) * 3,
        scratch_shapes=[
            pltpu.VMEM(field, BF16),
            pltpu.VMEM(field, BF16),
            pltpu.VMEM(columns(0), BF16),
            pltpu.VMEM((LAYERS, 9, channels, channels), BF16),
            pltpu.VMEM((LAYERS, 12 * channels, 2 * channels), BF16),
            pltpu.VMEM((LAYERS, 2 * channels, 12 * channels), BF16),
            pltpu.VMEM((width + 2 * max(LEVEL_PAD), rows + 2 * PAD, channels), F32),
            pltpu.VMEM(columns(0), BF16),
            *[pltpu.VMEM(columns(pad, 3), BF16) for pad in LEVEL_PAD],
            *[pltpu.VMEM(columns(pad, 3), BF16) for pad in SIGNAL_PAD],
            *[pltpu.VMEM(columns(pad), F32) for pad in SLOPE_PAD],
            pltpu.VMEM((LAYERS, ranks, 9 * block, channels), BF16),
            pltpu.VMEM((LAYERS, ranks, 9 * block, channels), BF16),
            pltpu.VMEM((2, groups, block, channels), BF16),
            pltpu.VMEM((2, groups, block, channels), BF16),
            pltpu.VMEM((width // 2, rows, 2 * channels), F32),
            pltpu.SemaphoreType.DMA((3,)),
            pltpu.SemaphoreType.DMA((len(PIECES), 2, 4)),
            pltpu.SemaphoreType.DMA((len(PIECES), 2, 4)),
            pltpu.SemaphoreType.DMA((LAYERS,)),
            pltpu.SemaphoreType.DMA((LAYERS,)),
            pltpu.SemaphoreType.DMA((2,)),
            pltpu.SemaphoreType.DMA((2,)),
            pltpu.SemaphoreType.REGULAR((2, 4)),
        ],
        compiler_params=pltpu.CompilerParams(
            collective_id=0, has_side_effects=True, vmem_limit_bytes=58 * 2**20
        ),
        name="panorama",
    )(images.reshape(field), weights, cotangent.reshape(field))
    features, input_grad, owned = pl.pallas_call(
        store,
        out_shape=(
            jax.ShapeDtypeStruct(field, BF16),
            jax.ShapeDtypeStruct(field, BF16),
            jax.ShapeDtypeStruct((LAYERS, block, share), F32),
        ),
        in_specs=[pl.BlockSpec(memory_space=pltpu.VMEM)] * 3,
        out_specs=[pl.BlockSpec(memory_space=pl.ANY)] * 3,
        scratch_shapes=[pltpu.SemaphoreType.DMA((3,))],
        name="store",
    )(*[pltpu.with_memory_space_constraint(x, pltpu.VMEM) for x in (features, input_grad, owned)])
    weight_grads = jnp.swapaxes(owned, 1, 2)
    return features.reshape(images.shape), input_grad.reshape(images.shape), weight_grads


def solution(mesh):
    return jax.shard_map(
        local,
        mesh=mesh,
        in_specs=(P("batch", None, "lon", None), P(), P("batch", None, "lon", None)),
        out_specs=(
            P("batch", None, "lon", None),
            P("batch", None, "lon", None),
            P(None, "lon", "batch"),
        ),
        check_vma=False,
    )
```

```python
import functools
import math

import jax
import jax.numpy as jnp
from jax import lax
from jax.experimental import pallas as pl
from jax.experimental.pallas import tpu as pltpu
from jax.sharding import PartitionSpec as P

LAYERS = 4
PAD = 8
BF16 = jnp.bfloat16
F32 = jnp.float32
MESH = pl.DeviceIdType.MESH

LEVEL_PAD = (7, 6, 4, 8)
SIGNAL_PAD = (1, 2, 6, 8)
SLOPE_PAD = (0, 2, 0)
PIECES = (
    (((0, 3), (3, 4)), ((13, 3), (9, 4))),
    (tuple((c, 1) for c in range(8)), tuple((c, 1) for c in range(8, 16))),
    (tuple((c, 1) for c in range(8)), tuple((c, 1) for c in range(8, 16))),
    (((0, 2), (4, 2), (2, 2)), ((12, 2), (10, 2), (14, 2))),
    (((0, 1),), ((15, 1),)),
)


def swapped(value):
    return jnp.swapaxes(value, 0, 1)


def kernel(
    ring, images_ref, weights_ref, cotangent_ref, features_ref, input_grad_ref, owned_ref, *scratch
):
    groups, ranks = ring
    (staged, upstream, columns_up, taps, forward_w, backward_w, shifter, slabs) = scratch[:8]
    levels = scratch[8:12]
    signals = scratch[12:16]
    slopes = scratch[16:19]
    send_b, recv_b, send_l, recv_l, partial, local_sem = scratch[19:25]
    halo_send, halo_recv, batch_send, batch_recv, lon_send, lon_recv, known = scratch[25:32]

    lon = lax.axis_index("lon")
    batch = lax.axis_index("batch")
    right, left = lax.rem(lon + 1, groups), lax.rem(lon + groups - 1, groups)
    rows, width, channels = staged.shape
    block = channels // ranks
    share = 9 * channels // groups

    barrier = pltpu.get_barrier_semaphore()
    axes = (("lon", lon, groups), ("batch", batch, ranks))

    def tell(semaphore, which, apart):
        name, here, size = axes[which]
        for peer in (lax.rem(here + apart, size), lax.rem(here + size - apart, size)):
            pl.semaphore_signal(semaphore, inc=1, device_id={name: peer}, device_id_type=MESH)

    def tell_round(turn):
        for which, (_, _, size) in enumerate(axes):
            if 4 * 2**turn <= size:
                tell(known.at[which, turn], which, 2**turn)

    def hear_round(turn):
        for which, (_, _, size) in enumerate(axes):
            if 4 * 2**turn <= size:
                pl.semaphore_wait(known.at[which, turn], 2)

    fetch_images = pltpu.make_async_copy(images_ref, staged, local_sem.at[0])
    fetch_taps = pltpu.make_async_copy(weights_ref, taps, local_sem.at[1])
    fetch_upstream = pltpu.make_async_copy(cotangent_ref, upstream, local_sem.at[2])
    fetch_images.start()
    tell(barrier, 0, 1)
    tell(barrier, 1, 1)
    fetch_taps.start()
    fetch_upstream.start()

    exchanged = (
        (levels[0], LEVEL_PAD[0]),
        (levels[3], LEVEL_PAD[3]),
        (signals[3], SIGNAL_PAD[3]),
        (signals[2], SIGNAL_PAD[2]),
        (signals[0], SIGNAL_PAD[0]),
    )

    def halo_copy(which, side, piece):
        buffer, pad = exchanged[which]
        first, count = PIECES[which][side][piece]
        landing = first + width if side == 0 else first - width
        return pltpu.make_async_remote_copy(
            src_ref=buffer.at[1, pad + first : pad + first + count],
            dst_ref=buffer.at[1, pad + landing : pad + landing + count],
            send_sem=halo_send.at[which, side, piece],
            recv_sem=halo_recv.at[which, side, piece],
            device_id={"lon": left if side == 0 else right},
            device_id_type=MESH,
        )

    def fill(buffer, dilation, slot, value):
        shifter[slot, pl.ds(PAD, rows), :] = value
        buffer[0, slot] = shifter[slot, pl.ds(PAD - dilation, rows), :].astype(BF16)
        buffer[2, slot] = shifter[slot, pl.ds(PAD + dilation, rows), :].astype(BF16)

    def receive(which, side, piece, dilation):
        buffer, pad = exchanged[which]
        halo_copy(which, side, piece).wait_recv()
        first, count = PIECES[which][side][piece]
        landing = pad + (first + width if side == 0 else first - width)
        for slot in range(landing, landing + count):
            fill(buffer, dilation, slot, buffer[1, slot].astype(F32))

    def tap_block(number, tap_row, tap_column, turned):
        if not 0 <= tap_column < 3:
            return jnp.zeros((channels, channels), BF16)
        tap = 3 * tap_row + tap_column
        return taps[number, 8 - tap if turned else tap]

    def build_forward(number):
        for span in range(4):
            for row in range(3):
                for side in range(2):
                    forward_w[
                        number,
                        pl.ds((3 * span + row) * channels, channels),
                        pl.ds(side * channels, channels),
                    ] = tap_block(number, row, span - side, False)

    def build_backward(number):
        for span in range(4):
            for row in range(3):
                for side in range(2):
                    backward_w[
                        number,
                        pl.ds(side * channels, channels),
                        pl.ds((3 * span + row) * channels, channels),
                    ] = tap_block(number, row, span - side, True)

    def gathered(buffer, pad, dilation, column, spans=range(4)):
        return jnp.concatenate(
            [
                buffer[row, pad + column + (span - 1) * dilation]
                for span in spans
                for row in range(3)
            ],
            axis=-1,
        )

    inner, outer = (1, 2), (0, 3)
    third = 3 * channels

    def forward_part(number, column, spans):
        return jnp.dot(
            gathered(levels[number], LEVEL_PAD[number], 2**number, column, spans),
            jnp.concatenate([forward_w[number, pl.ds(span * third, third), :] for span in spans], axis=0),
            preferred_element_type=F32,
        )

    def backward_part(number, column, spans, sides=2):
        return lax.dot_general(
            gathered(signals[number], SIGNAL_PAD[number], 2**number, column, spans),
            jnp.concatenate(
                [
                    backward_w[number, pl.ds(0, sides * channels), pl.ds(span * third, third)]
                    for span in spans
                ],
                axis=1,
            ),
            (((1,), (1,)), ((), ())),
            preferred_element_type=F32,
        )

    def forward_pair(number, column):
        dilation = 2**number
        if number + 1 < LAYERS:
            summed = forward_part(number, column, range(4))
        else:
            summed = partial[column] + forward_part(number, column, outer)
        for side in range(2):
            here = column + side * dilation
            z = summed[:, side * channels : (side + 1) * channels]
            sigma = 0.5 * jnp.tanh(0.5 * z) + 0.5
            act = z * sigma
            if number + 1 < LAYERS:
                if -SLOPE_PAD[number] <= here < width + SLOPE_PAD[number]:
                    slopes[number][SLOPE_PAD[number] + here] = sigma + act - act * sigma
                following, slot = levels[number + 1], LEVEL_PAD[number + 1] + here
                following[1, slot] = act.astype(BF16)
                fill(following, 2 * dilation, slot, act)
            else:
                slabs[here] = act.astype(BF16)
                signal = columns_up[here].astype(F32) * (sigma + act - act * sigma)
                slot = SIGNAL_PAD[number] + here
                signals[number][1, slot] = signal.astype(BF16)
                fill(signals[number], dilation, slot, signal)

    def backward_columns(number, column, sides):
        dilation = 2**number
        if number == 2 and sides == 2:
            outside = (0,) if column < dilation else (3,)
            back = partial[column % 8 + column // 8 * 4] + backward_part(number, column, outside)
        elif number + 1 < LAYERS:
            back = backward_part(number, column, range(2 + sides), sides)
        else:
            back = partial[column] + backward_part(number, column, outer)
        for side in range(sides):
            here = column + side * dilation
            value = back[:, side * channels : (side + 1) * channels]
            if number > 0:
                value = value * slopes[number - 1][SLOPE_PAD[number - 1] + here]
                slot = SIGNAL_PAD[number - 1] + here
                signals[number - 1][1, slot] = value.astype(BF16)
                fill(signals[number - 1], dilation // 2, slot, value)
            else:
                slabs[here] = value.astype(BF16)

    def weight_grad(number, cut=None):
        dilation = 2**number
        pad, level_pad = SIGNAL_PAD[number], LEVEL_PAD[number]
        signal = signals[number][1, pad : pad + width].reshape(rows * width, channels)
        for j in range(3):
            first = level_pad + (j - 1) * dilation
            taken = jnp.concatenate(
                [
                    levels[number][i, first : first + width].reshape(rows * width, channels)
                    for i in range(3)
                ],
                axis=-1,
            )
            total = lax.dot_general(
                signal, taken, (((0,), (0,)), ((), ())), preferred_element_type=F32
            ).astype(BF16)
            for i in range(3):
                send_b[number, :, pl.ds((3 * j + i) * block, block), :] = total[
                    :, i * channels : (i + 1) * channels
                ].reshape(ranks, block, channels)
            if cut is not None and j + 1 == cut:
                start_batch(number, 0, cut)
        start_batch(number, cut or 0, 3)

    def start_batch(number, first, last):
        half = ranks // 4
        for step in (half, 3 * half, *(n for n in range(1, ranks) if n not in (half, 3 * half))):
            target = lax.rem(batch + step, ranks)
            pltpu.make_async_remote_copy(
                src_ref=send_b.at[number, target, pl.ds(3 * first * block, 3 * (last - first) * block)],
                dst_ref=recv_b.at[number, step, pl.ds(3 * first * block, 3 * (last - first) * block)],
                send_sem=batch_send.at[number],
                recv_sem=batch_recv.at[number],
                device_id={"batch": target},
                device_id_type=MESH,
            ).start()

    sets = ((3, 2), (0, 1))

    lane = lax.broadcasted_iota(jnp.int32, (block, channels), 1)

    def start_lon(which):
        totals = []
        for number in sets[which]:
            arrived = recv_b.at[number, 1:]
            pltpu.make_async_copy(arrived, arrived, batch_recv.at[number]).wait()
            total = send_b[number, batch].astype(F32)
            for step in range(1, ranks):
                total = total + recv_b[number, step].astype(F32)
            totals.append(total)

        def shifted(total, tap, amount):
            place = 3 * (tap % 3) + tap // 3
            value = total[place * block : (place + 1) * block]
            return pltpu.roll(value, amount, 1) if amount else value

        for target in range(groups):
            tap, offset = divmod(target * share, channels)
            packed = None
            for place, total in enumerate(totals):
                amount = (place * share - offset) % channels
                value = shifted(total, tap, amount)
                if offset + share > channels:
                    more = shifted(total, tap + 1, amount)
                    value = jnp.where(lane < place * share + channels - offset, value, more)
                packed = value if packed is None else jnp.where(lane < place * share, packed, value)
            send_l[which, target] = packed.astype(BF16)

        @pl.loop(0, groups - 1)
        def _(turn):
            rank = turn // 2
            apart = ((rank + 1) // 2) * (2 * (rank % 2) - 1)
            step = (groups // 4 + (turn % 2) * (groups // 2) + apart + groups) % groups
            target = lax.rem(lon + step, groups)
            pltpu.make_async_remote_copy(
                src_ref=send_l.at[which, target],
                dst_ref=recv_l.at[which, step],
                send_sem=lon_send.at[which],
                recv_sem=lon_recv.at[which],
                device_id={"lon": target},
                device_id_type=MESH,
            ).start()

    def finish(which):
        arrived = recv_l.at[which, 1:]
        pltpu.make_async_copy(arrived, arrived, lon_recv.at[which]).wait()
        total = send_l[which, lon].astype(F32)
        for step in range(1, groups):
            total = total + recv_l[which, step].astype(F32)
        total = total * (1.0 / math.sqrt(rows * width * groups * ranks))
        for place, number in enumerate(sets[which]):
            owned_ref[number] = total[:, place * share : (place + 1) * share]

    fetch_images.wait()
    level, pad = levels[0], LEVEL_PAD[0]
    level[1, pad : pad + width] = swapped(staged[...])
    pl.semaphore_wait(barrier, 4)
    for piece in range(2):
        for side in range(2):
            halo_copy(0, side, piece).start()
    tell_round(0)
    edge_rows = jnp.zeros((PAD, channels), F32)
    for slot in range(shifter.shape[0]):
        shifter[slot, pl.ds(0, PAD), :] = edge_rows
        shifter[slot, pl.ds(PAD + rows, PAD), :] = edge_rows
    for column in range(width):
        fill(level, 1, pad + column, level[1, pad + column].astype(F32))
    fetch_taps.wait()
    build_forward(0)
    for column in range(2, width - 2, 2):
        forward_pair(0, column)
    build_forward(1)
    for column in (4, 5, 8, 9):
        forward_pair(1, column)
    fetch_upstream.wait()
    columns_up[...] = swapped(upstream[...])
    for number in (2, 3):
        build_forward(number)
    for number in range(LAYERS):
        build_backward(number)
    hear_round(0)
    tell_round(1)
    for half in range(2):
        receive(0, 0, half, 1)
        receive(0, 1, half, 1)
        for place in (2 * half, 2 * half + 1):
            forward_pair(0, -2 * place)
            forward_pair(0, width - 2 + 2 * place)
        for column in ((0, 1, 12, 13), (-4, -3, 16, 17))[half]:
            forward_pair(1, column)
    order = (0, 1, 4, 5, 2, 3, 6, 7)
    for half in range(2):
        for side in range(2):
            for column in (2 * half, 2 * half + 1):
                forward_pair(2, column + 8 * side)
            for piece in (2 * half, 2 * half + 1, 2 * half + 4, 2 * half + 5):
                halo_copy(1, side, piece).start()
    for column in range(8):
        partial[column] = forward_part(3, column, inner)
    hear_round(1)
    tell_round(2)
    for column in order:
        for side in range(2):
            receive(1, side, column, 8)
        forward_pair(3, column)
        for side in range(2):
            halo_copy(2, side, column).start()

    for column in range(8):
        partial[column] = backward_part(3, column, inner)
    features_ref[...] = swapped(slabs[...])
    ready = (((0, 0),), ((0, 1), (1, 0)), ((0, 2), (1, 1)), ((1, 2),))
    hear_round(2)
    tell_round(3)
    for place, column in enumerate(order):
        for side in range(2):
            receive(2, side, column, 8)
        backward_columns(3, column, 2)
        for side, part in ready[place // 2] if place % 2 else ():
            halo_copy(3, side, part).start()
    weight_grad(3)
    weight_grad(2)
    for column in (0, 1, 2, 3, 8, 9, 10, 11):
        partial[column % 8 + column // 8 * 4] = backward_part(
            2, column, (1, 2, 3) if column < 4 else (0, 1, 2)
        )
    for side in range(2):
        for piece in range(3):
            receive(3, side, piece, 4)
    for column in (0, 1, 2, 3, 8, 9, 10, 11):
        backward_columns(2, column, 2)
    for column in (-2, -1, 16, 17):
        backward_columns(2, column, 1)
    for column in (0, 13, 1, 4, 5, 8, 9, 12):
        backward_columns(1, column, 2)
        if column == 13:
            halo_copy(4, 0, 0).start()
            halo_copy(4, 1, 0).start()
    weight_grad(0)
    weight_grad(1, 2)
    hear_round(3)
    start_lon(0)
    start_lon(1)
    receive(4, 0, 0, 1)
    receive(4, 1, 0, 1)
    for column in range(0, width, 2):
        backward_columns(0, column, 2)
    input_grad_ref[...] = swapped(slabs[...])

    for which in range(len(PIECES)):
        for side in range(2):
            for piece in range(len(PIECES[which][side])):
                halo_copy(which, side, piece).wait_send()
    for number in range(LAYERS):
        sent = send_b.at[number, 1:]
        pltpu.make_async_copy(sent, sent, batch_send.at[number]).wait()
    finish(0)
    finish(1)
    for which in range(2):
        sent = send_l.at[which, 1:]
        pltpu.make_async_copy(sent, sent, lon_send.at[which]).wait()


def store(*refs):
    copies = [
        pltpu.make_async_copy(refs[n], refs[3 + n], refs[6].at[n]) for n in range(3)
    ]
    for copy in copies:
        copy.start()
    for copy in copies:
        copy.wait()


def local(images, weights, cotangent):
    _, rows, width, channels = images.shape
    groups, ranks = lax.axis_size("lon"), lax.axis_size("batch")
    block = channels // ranks
    share = 9 * channels // groups
    field = (rows, width, channels)

    def columns(pad, *front):
        return (*front, width + 2 * pad, rows, channels)

    features, input_grad, owned = pl.pallas_call(
        functools.partial(kernel, (groups, ranks)),
        out_shape=(
            pltpu.VMEM(field, BF16),
            pltpu.VMEM(field, BF16),
            pltpu.VMEM((LAYERS, block, share), F32),
        ),
        in_specs=[pl.BlockSpec(memory_space=pl.ANY)] * 3,
        out_specs=(pl.BlockSpec(memory_space=pltpu.VMEM),) * 3,
        scratch_shapes=[
            pltpu.VMEM(field, BF16),
            pltpu.VMEM(field, BF16),
            pltpu.VMEM(columns(0), BF16),
            pltpu.VMEM((LAYERS, 9, channels, channels), BF16),
            pltpu.VMEM((LAYERS, 12 * channels, 2 * channels), BF16),
            pltpu.VMEM((LAYERS, 2 * channels, 12 * channels), BF16),
            pltpu.VMEM((width + 2 * max(LEVEL_PAD), rows + 2 * PAD, channels), F32),
            pltpu.VMEM(columns(0), BF16),
            *[pltpu.VMEM(columns(pad, 3), BF16) for pad in LEVEL_PAD],
            *[pltpu.VMEM(columns(pad, 3), BF16) for pad in SIGNAL_PAD],
            *[pltpu.VMEM(columns(pad), F32) for pad in SLOPE_PAD],
            pltpu.VMEM((LAYERS, ranks, 9 * block, channels), BF16),
            pltpu.VMEM((LAYERS, ranks, 9 * block, channels), BF16),
            pltpu.VMEM((2, groups, block, channels), BF16),
            pltpu.VMEM((2, groups, block, channels), BF16),
            pltpu.VMEM((width // 2, rows, 2 * channels), F32),
            pltpu.SemaphoreType.DMA((3,)),
            pltpu.SemaphoreType.DMA((len(PIECES), 2, 8)),
            pltpu.SemaphoreType.DMA((len(PIECES), 2, 8)),
            pltpu.SemaphoreType.DMA((LAYERS,)),
            pltpu.SemaphoreType.DMA((LAYERS,)),
            pltpu.SemaphoreType.DMA((2,)),
            pltpu.SemaphoreType.DMA((2,)),
            pltpu.SemaphoreType.REGULAR((2, 4)),
        ],
        compiler_params=pltpu.CompilerParams(
            collective_id=0, has_side_effects=True, vmem_limit_bytes=58 * 2**20
        ),
        name="panorama",
    )(images.reshape(field), weights, cotangent.reshape(field))
    features, input_grad, owned = pl.pallas_call(
        store,
        out_shape=(
            jax.ShapeDtypeStruct(field, BF16),
            jax.ShapeDtypeStruct(field, BF16),
            jax.ShapeDtypeStruct((LAYERS, block, share), F32),
        ),
        in_specs=[pl.BlockSpec(memory_space=pltpu.VMEM)] * 3,
        out_specs=[pl.BlockSpec(memory_space=pl.ANY)] * 3,
        scratch_shapes=[pltpu.SemaphoreType.DMA((3,))],
        name="store",
    )(*[pltpu.with_memory_space_constraint(x, pltpu.VMEM) for x in (features, input_grad, owned)])
    weight_grads = jnp.swapaxes(owned, 1, 2)
    return features.reshape(images.shape), input_grad.reshape(images.shape), weight_grads


def solution(mesh):
    return jax.shard_map(
        local,
        mesh=mesh,
        in_specs=(P("batch", None, "lon", None), P(), P("batch", None, "lon", None)),
        out_specs=(
            P("batch", None, "lon", None),
            P("batch", None, "lon", None),
            P(None, "lon", "batch"),
        ),
        check_vma=False,
    )
```
